256 devices in a mesh: clip: 16 (over z_hi, y), seq: 16 (over x, z_lo, core).
Axes of the slice: x: 4, y: 4, z: 8 (z_hi: 4, z_lo: 2; z = z_hi * 2 + z_lo), core: 2. Of those that a mesh axis runs over, the one named last changes fastest.
Arguments:
- space_query: bfloat16 [16, 16, 256, 1152], P('clip', 'seq'), may hold values from -2.5 to 2.5
- space_keys: bfloat16 [16, 16, 256, 1152], P('clip', 'seq'), may hold values from -2.5 to 2.5
- space_values: bfloat16 [16, 16, 256, 1152], P('clip', 'seq'), may hold values from -6 to 6
- space_output: bfloat16 [16, 16, 256, 1152], P('clip', 'seq'), may hold values from -6 to 6
- space_logsum: float32 [16, 16, 16, 256], P('clip', 'seq'), may hold values from 4.5 to 6.5
- time_query: bfloat16 [16, 16, 256, 1152], P('clip', 'seq'), may hold values from -2.5 to 2.5
- time_keys: bfloat16 [16, 16, 256, 1152], P('clip', 'seq'), may hold values from -2.5 to 2.5
- time_values: bfloat16 [16, 16, 256, 1152], P('clip', 'seq'), may hold values from -6 to 6
- time_output: bfloat16 [16, 16, 256, 1152], P('clip', 'seq'), may hold values from -6 to 6
- time_logsum: float32 [16, 256, 16, 16], P('clip', 'seq'), may hold values from 2 to 4
- upstream: bfloat16 [16, 16, 256, 1152], P('clip', 'seq'), may hold values from -6 to 6
- space_weight: bfloat16 [1152, 1152], P('seq'), may hold values from -0.1875 to 0.1875
- time_weight: bfloat16 [1152, 1152], P('seq'), may hold values from -0.1875 to 0.1875
Outputs:
- dquery_space: bfloat16 [16, 16, 256, 1152], P('clip', 'seq')
- dkeys_space: bfloat16 [16, 16, 256, 1152], P('clip', 'seq')
- dvalue_space: bfloat16 [16, 16, 256, 1152], P('clip', 'seq')
- dquery_time: bfloat16 [16, 16, 256, 1152], P('clip', 'seq')
- dkeys_time: bfloat16 [16, 16, 256, 1152], P('clip', 'seq')
- dvalue_time: bfloat16 [16, 16, 256, 1152], P('clip', 'seq')
- dweight_space: float32 [1152, 1152], P('seq', 'clip')
- dweight_time: float32 [1152, 1152], P('seq', 'clip')
The draws below stay inside these ranges and needn't reach their ends.
All inputs are finite; a program needn't handle non-finite values.
Results may differ from the reference program's by a relative error of at most 0.006.
Values may be sent and summed in bfloat16 or wider, within the bound.
A program may use at most 192 MiB of HBM per device.

```python
import math
import jax
import jax.numpy as jnp
from jax import lax

HEADS = 16
D = 1152
S = 256
FRAMES = 16
CLIPS = 16


def raised(values, own_key, source, target, blocks, factor):
    def block_of(dim):
        return (jnp.arange(values.shape[dim]) // (values.shape[dim] // blocks)).reshape((-1,) + (1,) * (values.ndim - 1 - dim))

    one_side = jax.random.permutation(own_key, blocks)[block_of(target)]
    second = (block_of(target) + blocks // 2) % blocks
    return jnp.where((block_of(source) == one_side) | (block_of(source) == second), factor * values, values)


def level_of(rng, dims, shards, low, top_value):
    factor_of, own = 1.0, jax.random.fold_in(rng, 6)
    for dim, shards_of in shards:
        draws = jnp.exp(jax.random.uniform(jax.random.fold_in(own, dim), (shards_of,), jnp.float32, low / len(shards), top_value / len(shards)))
        factor_of = factor_of * jnp.repeat(draws, dims[dim] // shards_of).reshape([-1 if axis == dim else 1 for axis in range(len(dims))])
    return factor_of


def centred(rng, dims, width, reach, split=(), dtype=jnp.bfloat16):
    values = jax.random.normal(rng, dims, jnp.float32) * width
    if len(split) > 0:
        values = level_of(rng, dims, split, -0.22, 0.18) * values
    return jnp.clip(values, min=-reach, max=reach).astype(dtype)


def bell_draw_with(key, extent, scale, reach, split, heavy, held_as=jnp.bfloat16):
    values = scale * jax.random.normal(key, extent, jnp.float32)
    if split:
        values = values * level_of(key, extent, split, -0.22, 0.18)
    return jnp.clip(raised(values, jax.random.fold_in(key, 3), *heavy), -reach, reach).astype(held_as)


def setup_inputs(seed: int = 0) -> dict:
    key_of = jax.random.split(jax.random.key(seed), 14)
    return {
        "space_query": centred(key_of[0], (CLIPS, FRAMES, S, D), 0.7, 2.5, ((0, 16), (1, 16))),
        "space_keys": centred(key_of[1], (CLIPS, FRAMES, S, D), 0.7, 2.5, ((0, 16), (1, 16))),
        "space_values": centred(key_of[2], (CLIPS, FRAMES, S, D), 1.0, 6.0, ((0, 16), (1, 16))),
        "space_output": bell_draw_with(key_of[3], (CLIPS, FRAMES, S, D), 1.0, 6.0, ((0, 16), (1, 16)), (1, 3, 16, 2.0)),
        "space_logsum": jnp.clip(4.5 + 2.0 * jax.random.uniform(key_of[4], (CLIPS, FRAMES, HEADS, S), jnp.float32) ** level_of(key_of[4], (CLIPS, FRAMES, HEADS, S), ((0, 16), (1, 16)), -0.2, 0.2), 4.5, 6.5),
        "time_query": centred(key_of[5], (CLIPS, FRAMES, S, D), 0.7, 2.5, ((0, 16), (1, 16))),
        "time_keys": centred(key_of[6], (CLIPS, FRAMES, S, D), 0.7, 2.5, ((0, 16), (1, 16))),
        "time_values": centred(key_of[7], (CLIPS, FRAMES, S, D), 1.0, 6.0, ((0, 16), (1, 16))),
        "time_output": bell_draw_with(key_of[8], (CLIPS, FRAMES, S, D), 1.0, 6.0, ((0, 16), (1, 16)), (1, 3, 16, 2.0)),
        "time_logsum": jnp.clip(2.0 + 2.0 * jax.random.uniform(key_of[9], (CLIPS, S, HEADS, FRAMES), jnp.float32) ** level_of(key_of[9], (CLIPS, S, HEADS, FRAMES), ((0, 16), (1, 16)), -0.2, 0.2), 2.0, 4.0),
        "upstream": bell_draw_with(key_of[10], (CLIPS, FRAMES, S, D), 1.0, 6.0, ((0, 16), (1, 16)), (0, 3, 16, 2.0)),
        "space_weight": centred(key_of[11], (D, D), D ** -0.5, 0.1875, ((0, 16),)),
        "time_weight": centred(key_of[12], (D, D), D ** -0.5, 0.1875, ((0, 16),)),
    }


def attention_terms(queries, key_rows, values, outputs, cotangent, logsum):
    head_count = logsum.shape[1]
    length, batch, features = queries.shape
    head_dim = features // head_count
    factor = 1.0 / math.sqrt(head_dim)
    shape = (length, batch, head_count, head_dim)
    query_split = queries.reshape(shape).astype(jnp.float32)
    key_split = key_rows.reshape(shape).astype(jnp.float32)
    value_split = values.reshape(shape).astype(jnp.float32)
    output_split = outputs.reshape(shape).astype(jnp.float32)
    grad_split = cotangent.reshape(shape).astype(jnp.float32)
    scores = jnp.einsum('ibhe,jbhe->bhij', query_split, key_split) * factor
    attention_probs = jnp.exp(scores - logsum[:, :, :, None])
    probs_low = lax.optimization_barrier(attention_probs.astype(jnp.bfloat16)).astype(jnp.float32)
    center = jnp.einsum('ibhe,ibhe->bhi', grad_split, output_split)
    dvalue = jnp.einsum('bhij,ibhe->jbhe', probs_low, grad_split).astype(jnp.bfloat16)
    dprob = jnp.einsum('ibhe,jbhe->bhij', grad_split, value_split)
    dscore = (attention_probs * (dprob - center[:, :, :, None]) * factor).astype(jnp.bfloat16)
    dscore_wide = lax.optimization_barrier(dscore).astype(jnp.float32)
    dquery = jnp.einsum('bhij,jbhe->ibhe', dscore_wide, key_split).astype(jnp.bfloat16)
    dkeys = jnp.einsum('bhij,ibhe->jbhe', dscore_wide, query_split).astype(jnp.bfloat16)
    flat = (length, batch, features)
    return (dquery.reshape(flat), dkeys.reshape(flat), dvalue.reshape(flat))

def reference(space_query, space_keys, space_values, space_output, space_logsum, time_query, time_keys, time_values, time_output, time_logsum, upstream, space_weight, time_weight):
    features = upstream.shape[3]
    full_shape = upstream.shape
    flat_up = upstream.reshape(-1, features)
    space_grad = jnp.dot(flat_up, space_weight.T, preferred_element_type=jnp.float32).astype(jnp.bfloat16).reshape(full_shape)
    time_grad = jnp.dot(flat_up, time_weight.T, preferred_element_type=jnp.float32).astype(jnp.bfloat16).reshape(full_shape)

    def space_item(items):
        return attention_terms(items[0][:, None, :], items[1][:, None, :], items[2][:, None, :], items[3][:, None, :], items[4][:, None, :], items[5][None])
    space_inputs = tuple((array.reshape(CLIPS * FRAMES, S, features) for array in (space_query, space_keys, space_values, space_output, space_grad)))
    space_inputs = space_inputs + (space_logsum.reshape(CLIPS * FRAMES, HEADS, S),)
    space_results = lax.map(space_item, space_inputs)
    dquery_space, dkeys_space, dvalue_space = tuple((result.reshape(full_shape) for result in space_results))

    def time_item(items):
        return attention_terms(items[0], items[1], items[2], items[3], items[4], items[5])
    time_results = lax.map(time_item, (time_query, time_keys, time_values, time_output, time_grad, time_logsum))
    dquery_time, dkeys_time, dvalue_time = tuple((result.reshape(full_shape) for result in time_results))
    factor = 1.0 / math.sqrt(CLIPS * FRAMES * S)
    dweight_space = jnp.dot(space_output.reshape(-1, features).T, flat_up, preferred_element_type=jnp.float32) * factor
    dweight_time = jnp.dot(time_output.reshape(-1, features).T, flat_up, preferred_element_type=jnp.float32) * factor
    return (dquery_space, dkeys_space, dvalue_space, dquery_time, dkeys_time, dvalue_time, dweight_space, dweight_time)
```

```python
import math

import jax
import jax.numpy as jnp
from jax import lax
from jax.experimental import pallas as pl
from jax.experimental.pallas import tpu as pltpu
from jax.sharding import PartitionSpec as P

BF16 = jnp.bfloat16
F32 = jnp.float32
HEADS = 16
HEAD = 72
D = HEADS * HEAD
S = 256
SEQ = 16
POS = S // SEQ
CHIPS = 8
YS = 4
ZHS = 4
CHIP_ROWS = 2 * HEAD
YROWS = ZHS * HEAD
WIDE = 384
GROUPS = ((0, 6), (6, 11), (11, 16))
FORWARD = ((0, 512), (512, 896), (896, 1152))
BACK = ((0, 384), (384, 768), (768, 1152))
NT = (((1,), (1,)), ((), ()))
TN = (((0,), (0,)), ((), ()))
NN = (((1,), (0,)), ((), ()))


def mm(a, b, dims):
    return lax.dot_general(a, b, dims, preferred_element_type=F32)


def kernel(
    up, tq, tk, tv, so, to, sq, sk, sv, ws, wt, slog, tlog,
    osq, osk, osv, otq, otk, otv, ows, owt,
    X, R, O, SI, GT, GS, TD, TE, SD, W, wown, w32, w32r,
    ind, bias, cen, cenr, cent, cens,
    ut, utp, mine, psend, prec, ysend, yrecv, xzsend, xzrecv, zs, zr,
    ld, own_sem, wp_s, wp_r, w1_s, w1_r, lf_s, lf_r, w2_s, w2_r, w3_s, w3_r, l3_s, l3_r,
    a_s, a_r, c_s, c_r, b_s, b_r, pp_s, pp_r, y_s, y_r, xz_s, xz_r, z_s, z_r, out_sem,
):
    clip = lax.axis_index("clip")
    seq = lax.axis_index("seq")
    y = lax.rem(clip, YS)
    zh = lax.div(clip, YS)
    core = lax.rem(seq, 2)
    chip = lax.div(seq, 2)
    sibling = seq + 1 - 2 * core
    corner = zh * 2 + core

    def seq_peer(k):
        return lax.rem(seq + k, SEQ)

    def chip_peer(k):
        return 2 * lax.rem(chip + k, CHIPS) + core

    def y_peer(k):
        return zh * YS + lax.rem(y + k, YS)

    def z_peer(k):
        other = lax.rem(corner + k, 2 * ZHS)
        return lax.div(other, 2), lax.rem(other, 2)

    def remote(src, dst, send, recv, **where):
        return pltpu.make_async_remote_copy(
            src_ref=src, dst_ref=dst, send_sem=send, recv_sem=recv,
            device_id=where, device_id_type=pl.DeviceIdType.MESH,
        )

    def drain(ref, sem):
        pltpu.make_async_copy(ref, ref, sem).wait()

    barrier = pltpu.get_barrier_semaphore()
    for k in range(1, SEQ):
        pl.semaphore_signal(barrier, inc=1, device_id={"seq": seq_peer(k)}, device_id_type=pl.DeviceIdType.MESH)
    for k in range(1, YS):
        pl.semaphore_signal(barrier, inc=1, device_id={"clip": y_peer(k)}, device_id_type=pl.DeviceIdType.MESH)
    for k in range(1, 2 * ZHS):
        to_zh, to_core = z_peer(k)
        pl.semaphore_signal(
            barrier, inc=1, device_id={"clip": to_zh * YS + y, "seq": 2 * chip + to_core},
            device_id_type=pl.DeviceIdType.MESH,
        )

    loads = [
        pltpu.make_async_copy(src, dst, ld.at[n])
        for n, (src, dst) in enumerate((
            (up, X.at[0]), (tq, X.at[1]), (tk, X.at[2]), (tv, X.at[3]), (so, O.at[0]), (to, O.at[1]),
            (sq, SI.at[0]), (sk, SI.at[1]), (sv, SI.at[2]),
        ))
    ]
    for load in loads:
        load.start()
    w32[0] = wt[...].astype(F32)
    w32[1] = ws[...].astype(F32)

    pl.semaphore_wait(barrier, (SEQ - 1) + (YS - 1) + (2 * ZHS - 1))

    pair = remote(w32, w32r, wp_s, wp_r, seq=sibling)
    pair.start()

    loads[0].wait()
    row_me = pl.ds(pl.multiple_of(seq * POS, POS), POS)

    def rows_of(d):
        return pl.ds(pl.multiple_of(d * POS, POS), POS)

    def send_up(k, carry):
        d = seq_peer(k)
        remote(X.at[0, rows_of(d)], R.at[0, row_me], a_s.at[0], a_r.at[0], seq=d).start()
        return carry

    lax.fori_loop(1, SEQ, send_up, 0)
    own_up = pltpu.make_async_copy(X.at[0, row_me], R.at[0, row_me], own_sem.at[0])
    own_up.start()

    head_row = lax.broadcasted_iota(jnp.int32, (128, D), 0) * HEAD
    column = lax.broadcasted_iota(jnp.int32, (128, D), 1)
    ind[...] = jnp.where((column >= head_row) & (column < head_row + HEAD), 1.0, 0.0).astype(BF16)

    pair.wait()
    chip_rows = pl.ds(pl.multiple_of(chip * CHIP_ROWS, 16), CHIP_ROWS)
    tile = pl.ds(pl.multiple_of((2 * y + core) * 128, 128), 128)
    last = pl.ds(D - 128, 128)
    for m in range(2):
        first, second = w32[m], w32r[m]
        low = jnp.where(core == 0, first, second)
        high = jnp.where(core == 0, second, first)
        wown[m] = jnp.concatenate((low, high), axis=0).astype(BF16)
    def stage1(m):
        W[m, chip_rows, tile] = wown[m, :, tile]

        def one(k, carry):
            remote(wown.at[m, :, tile], W.at[m, chip_rows, tile], w1_s.at[m], w1_r.at[m], seq=chip_peer(k)).start()
            return carry

        lax.fori_loop(1, CHIPS, one, 0)

    stage1(0)
    W[core, chip_rows, last] = wown[core, :, last]

    def send_last(k, carry):
        remote(wown.at[core, :, last], W.at[core, chip_rows, last], lf_s, lf_r, seq=chip_peer(k)).start()
        return carry

    lax.fori_loop(1, CHIPS, send_last, 0)

    for n in (1, 2, 3):
        loads[n].wait()
    for g, (begin, end) in enumerate(FORWARD):
        columns = pl.ds(begin, end - begin)

        def send_group(k, carry, g=g, columns=columns):
            d = seq_peer(k)
            remote(
                X.at[1:4, rows_of(d), columns], R.at[1:4, row_me, columns], a_s.at[1 + g], a_r.at[1 + g], seq=d
            ).start()
            return carry

        lax.fori_loop(1, SEQ, send_group, 0)
    own_rest = pltpu.make_async_copy(X.at[1:4, row_me], R.at[1:4, row_me], own_sem.at[1])
    own_rest.start()
    stage1(1)

    for n in range(D // 128):
        ut[128 * n:128 * (n + 1), :] = X[0, :, 128 * n:128 * (n + 1)].astype(F32).T
    for j in range(YS):
        utp[j] = jnp.concatenate(
            [ut[HEAD * (YS * i + j):HEAD * (YS * i + j + 1), :] for i in range(ZHS)], axis=0
        ).astype(BF16)
    loads[4].wait()
    loads[5].wait()
    factor = 1.0 / math.sqrt(lax.axis_size("clip") * SEQ * S)

    def gradient(k):
        rows = utp[lax.rem(y + k, YS)]

        def piece(n, carry):
            columns = pl.ds(pl.multiple_of(n * WIDE, 128), WIDE)
            psend[k, :, columns] = (mm(rows, O[1 - core, :, columns], NN) * factor).astype(BF16)
            mine[k, :, columns] = mm(rows, O[core, :, columns], NN) * factor
            return carry

        lax.fori_loop(0, D // WIDE, piece, 0)
        remote(psend.at[k], prec.at[k], pp_s.at[k], pp_r.at[k], seq=sibling).start()

    def stage2(m):
        drain(W.at[m, 0:(CHIPS - 1) * CHIP_ROWS, 0:128], w1_r.at[m])
        remote(W.at[m, :, tile], W.at[m, :, tile], w3_s.at[m], w3_r.at[m], seq=sibling).start()
        for k in range(1, YS):
            remote(W.at[m, :, tile], W.at[m, :, tile], w2_s.at[m], w2_r.at[m], clip=y_peer(k)).start()

    def stage3(m):
        drain(W.at[m, :, 0:384], w2_r.at[m])
        for k in range(1, YS):
            there = pl.ds(pl.multiple_of((2 * lax.rem(y + k, YS) + core) * 128, 128), 128)
            remote(W.at[m, :, there], W.at[m, :, there], w3_s.at[m], w3_r.at[m], seq=sibling).start()
        drain(W.at[m, :, 0:512], w3_r.at[m])

    gradient(2)
    stage2(0)
    drain(W.at[0, 0:(CHIPS - 1) * CHIP_ROWS, 0:128], lf_r)
    remote(W.at[core, :, last], W.at[core, :, last], l3_s, l3_r, seq=sibling).start()
    gradient(1)
    gradient(3)
    for k in (2, 1, 3):
        drain(prec.at[k], pp_r.at[k])
        ysend[k - 1] = (mine[k] + prec[k].astype(F32)).astype(BF16)
        remote(ysend.at[k - 1], yrecv.at[k - 1], y_s.at[k - 1], y_r.at[k - 1], clip=y_peer(k)).start()
    gradient(0)
    stage2(1)

    zeros = jnp.zeros((S, D), BF16)
    for n in range(3):
        TD[n] = zeros
        SD[n] = zeros
    position = lax.broadcasted_iota(jnp.int32, (S, S), 0)
    other = lax.broadcasted_iota(jnp.int32, (S, S), 1)
    bias[...] = jnp.where(lax.rem(position, POS) == lax.rem(other, POS), 0.0, -1e30)

    stage3(0)
    drain(W.at[0, :, last], l3_r)

    def project(tokens, m, n):
        return mm(tokens, W[m, n * WIDE:(n + 1) * WIDE, :], NT).astype(BF16)

    def split(grad, outputs):
        product = grad.astype(F32) * outputs.astype(F32)
        high = product.astype(BF16)
        return high, (product - high.astype(F32)).astype(BF16)

    total = jnp.zeros((S, 128), F32)
    for n in range(D // WIDE):
        columns = slice(n * WIDE, (n + 1) * WIDE)
        high, low = split(project(X[0], 0, n), O[1, :, columns])
        total = total + (mm(high, ind[:, columns], NT) + mm(low, ind[:, columns], NT))
    cen[...] = total

    def send_center(k, carry):
        d = seq_peer(k)
        remote(cen.at[rows_of(d)], cenr.at[row_me], c_s, c_r, seq=d).start()
        return carry

    lax.fori_loop(1, SEQ, send_center, 0)
    own_cen = pltpu.make_async_copy(cen.at[row_me], cenr.at[row_me], own_sem.at[2])
    own_cen.start()

    others = (SEQ - 1) * POS
    own_up.wait()
    drain(R.at[0, 0:others], a_r.at[0])
    for n in range(D // WIDE):
        GT[:, n * WIDE:(n + 1) * WIDE] = project(R[0], 0, n)
    own_cen.wait()
    drain(cenr.at[0:others], c_r)
    cent[...] = cenr[...].T

    scale = 1.0 / math.sqrt(HEAD)
    lane = lax.broadcasted_iota(jnp.int32, (16, 256), 1)

    def heads(first, end, q_ref, k_ref, v_ref, g_ref, log_ref, center_ref, masked, out):
        def one(h, carry):
            offset = jnp.minimum(lax.div(h * HEAD, 128), D // 128 - 2) * 128
            window = pl.ds(pl.multiple_of(offset, 128), 256)
            begin = h * HEAD - offset
            keep = jnp.where((lane >= begin) & (lane < begin + HEAD), 1.0, 0.0).astype(BF16)
            keep = jnp.broadcast_to(keep[None], (S // 16, 16, 256)).reshape(S, 256)
            q = q_ref[:, window] * keep
            g = g_ref[:, window] * keep
            k = k_ref[:, window]
            v = v_ref[:, window]
            scores = mm(k, q, NT) * scale - log_ref[pl.ds(h, 1), :]
            if masked:
                scores = scores + bias[...]
            probs = jnp.exp(scores)
            dscore = (probs * (mm(v, g, NT) - center_ref[pl.ds(h, 1), :]) * scale).astype(BF16)
            out[0, :, window] = out[0, :, window] + mm(dscore, k * keep, TN).astype(BF16)
            out[1, :, window] = out[1, :, window] + mm(dscore, q, NN).astype(BF16)
            out[2, :, window] = out[2, :, window] + mm(probs.astype(BF16), g, NN).astype(BF16)
            return carry

        lax.fori_loop(first, end, one, 0)

    own_rest.wait()
    own_back = []
    for n, ((first, end), (begin, stop), (low, top)) in enumerate(zip(GROUPS, FORWARD, BACK)):
        drain(R.at[1:4, 0:others, begin:stop], a_r.at[1 + n])
        heads(first, end, R.at[1], R.at[2], R.at[3], GT, tlog, cent, True, TD)
        columns = pl.ds(low, top - low)

        def send_back(k, carry, n=n, columns=columns):
            d = seq_peer(k)
            remote(TD.at[:, rows_of(d), columns], TE.at[:, row_me, columns], b_s.at[n], b_r.at[n], seq=d).start()
            return carry

        lax.fori_loop(1, SEQ, send_back, 0)
        back = pltpu.make_async_copy(TD.at[:, row_me, columns], TE.at[:, row_me, columns], own_sem.at[3 + n])
        back.start()
        own_back.append(back)

    drain(prec.at[0], pp_r.at[0])
    for k in range(1, YS):
        drain(yrecv.at[k - 1], y_r.at[k - 1])
    for n in range(D // 128):
        columns = slice(128 * n, 128 * (n + 1))
        held = mine[0, :, columns] + prec[0, :, columns].astype(F32)
        for k in range(YS - 1):
            held = held + yrecv[k, :, columns].astype(F32)
        held = jnp.concatenate((held, jnp.zeros((WIDE - YROWS, 128), F32)), axis=0)
        xzsend[128 * n:128 * (n + 1), :] = held.T.astype(BF16)
    for k in range(1, CHIPS):
        there = pl.ds(pl.multiple_of(lax.rem(chip + k, CHIPS) * CHIP_ROWS, 16), CHIP_ROWS)
        remote(xzsend.at[there], xzrecv.at[k - 1], xz_s, xz_r, seq=chip_peer(k)).start()

    stage3(1)
    total = jnp.zeros((128, S), F32)
    for n in range(D // WIDE):
        columns = slice(n * WIDE, (n + 1) * WIDE)
        grad = project(X[0], 1, n)
        GS[:, columns] = grad
        high, low = split(grad, O[0, :, columns])
        total = total + (mm(ind[:, columns], high, NT) + mm(ind[:, columns], low, NT))
    cens[...] = total
    for n in (6, 7, 8):
        loads[n].wait()
    heads(0, HEADS, SI.at[0], SI.at[1], SI.at[2], GS, slog, cens, False, SD)
    writes = [
        pltpu.make_async_copy(SD.at[n], ref, out_sem.at[n]) for n, ref in enumerate((osq, osk, osv))
    ]
    for write in writes:
        write.start()

    drain(xzrecv, xz_r)
    held = xzsend[chip_rows, :].astype(F32)
    for k in range(CHIPS - 1):
        held = held + xzrecv[k].astype(F32)
    for i in range(ZHS):
        moved = pltpu.roll(held, WIDE - HEAD * i, axis=1) if i else held
        for c in range(2):
            zs[2 * i + c] = moved[HEAD * c:HEAD * (c + 1), 0:128]
    slot = core * ZHS + zh
    for k in range(1, 2 * ZHS):
        to_zh, to_core = z_peer(k)
        remote(
            zs.at[2 * to_zh + to_core], zr.at[slot], z_s, z_r, clip=to_zh * YS + y, seq=2 * chip + to_core
        ).start()
    zr[slot] = zs[corner]

    for n, (low, top) in enumerate(BACK):
        own_back[n].wait()
        drain(TE.at[:, 0:others, low:top], b_r.at[n])
    for n, ref in enumerate((otq, otk, otv)):
        write = pltpu.make_async_copy(TE.at[n], ref, out_sem.at[3 + n])
        write.start()
        writes.append(write)

    drain(zr.at[0:2 * ZHS - 1], z_r)
    ows[...] = (zr[0] + zr[1] + zr[2] + zr[3])[:, 0:HEAD]
    owt[...] = (zr[4] + zr[5] + zr[6] + zr[7])[:, 0:HEAD]

    drain(X.at[0, 0:others], a_s.at[0])
    for n, (begin, stop) in enumerate(FORWARD):
        drain(X.at[1:4, 0:others, begin:stop], a_s.at[1 + n])
    for n, (low, top) in enumerate(BACK):
        drain(TD.at[:, 0:others, low:top], b_s.at[n])
    for m in range(2):
        drain(W.at[m, 0:(CHIPS - 1) * CHIP_ROWS, 0:128], w1_s.at[m])
        drain(W.at[m, :, 0:384], w2_s.at[m])
        drain(W.at[m, :, 0:512], w3_s.at[m])
    drain(W.at[0, 0:(CHIPS - 1) * CHIP_ROWS, 0:128], lf_s)
    drain(W.at[0, :, 0:128], l3_s)
    drain(cen.at[0:others], c_s)
    for k in range(YS):
        drain(psend.at[k], pp_s.at[k])
    for k in range(YS - 1):
        drain(ysend.at[k], y_s.at[k])
    drain(xzsend.at[0:(CHIPS - 1) * CHIP_ROWS], xz_s)
    drain(zs.at[0:2 * ZHS - 1], z_s)
    for write in writes:
        write.wait()


def shards(
    space_query, space_keys, space_values, space_output, space_logsum,
    time_query, time_keys, time_values, time_output, time_logsum,
    upstream, space_weight, time_weight,
):
    flat = (S, D)
    time_log = time_logsum.reshape(POS, HEADS, SEQ).transpose(1, 2, 0).reshape(HEADS, S)
    dma = pltpu.SemaphoreType.DMA
    big = jax.ShapeDtypeStruct(flat, BF16)
    small = jax.ShapeDtypeStruct((HEAD, HEAD), F32)
    anywhere = pl.BlockSpec(memory_space=pl.ANY)
    held = pl.BlockSpec(memory_space=pltpu.VMEM)
    results = pl.pallas_call(
        kernel,
        out_shape=(big,) * 6 + (small,) * 2,
        in_specs=[anywhere] * 9 + [held] * 4,
        out_specs=(anywhere,) * 6 + (held,) * 2,
        scratch_shapes=[
            pltpu.VMEM((4, S, D), BF16),
            pltpu.VMEM((4, S, D), BF16),
            pltpu.VMEM((2, S, D), BF16),
            pltpu.VMEM((3, S, D), BF16),
            pltpu.VMEM((S, D), BF16),
            pltpu.VMEM((S, D), BF16),
            pltpu.VMEM((3, S, D), BF16),
            pltpu.VMEM((3, S, D), BF16),
            pltpu.VMEM((3, S, D), BF16),
            pltpu.VMEM((2, D, D), BF16),
            pltpu.VMEM((2, CHIP_ROWS, D), BF16),
            pltpu.VMEM((2, HEAD, D), F32),
            pltpu.VMEM((2, HEAD, D), F32),
            pltpu.VMEM((128, D), BF16),
            pltpu.VMEM((S, S), F32),
            pltpu.VMEM((S, 128), F32),
            pltpu.VMEM((S, 128), F32),
            pltpu.VMEM((128, S), F32),
            pltpu.VMEM((128, S), F32),
            pltpu.VMEM((D, S), F32),
            pltpu.VMEM((YS, YROWS, S), BF16),
            pltpu.VMEM((YS, YROWS, D), F32),
            pltpu.VMEM((YS, YROWS, D), BF16),
            pltpu.VMEM((YS, YROWS, D), BF16),
            pltpu.VMEM((YS - 1, YROWS, D), BF16),
            pltpu.VMEM((YS - 1, YROWS, D), BF16),
            pltpu.VMEM((D, WIDE), BF16),
            pltpu.VMEM((CHIPS - 1, CHIP_ROWS, WIDE), BF16),
            pltpu.VMEM((2 * ZHS, HEAD, 128), F32),
            pltpu.VMEM((2 * ZHS, HEAD, 128), F32),
            dma((9,)), dma((6,)), dma, dma, dma((2,)), dma((2,)), dma, dma,
            dma((2,)), dma((2,)), dma((2,)), dma((2,)), dma, dma,
            dma((4,)), dma((4,)), dma, dma, dma((3,)), dma((3,)), dma((4,)), dma((4,)),
            dma((3,)), dma((3,)), dma, dma, dma, dma, dma((6,)),
        ],
        compiler_params=pltpu.CompilerParams(
            collective_id=0, has_side_effects=True, vmem_limit_bytes=60 * 1024 * 1024
        ),
        cost_estimate=pl.CostEstimate(flops=7_000_000_000, bytes_accessed=12_000_000, transcendentals=2_100_000),
    )(
        upstream.reshape(flat), time_query.reshape(flat), time_keys.reshape(flat), time_values.reshape(flat),
        space_output.reshape(flat), time_output.reshape(flat),
        space_query.reshape(flat), space_keys.reshape(flat), space_values.reshape(flat),
        space_weight, time_weight, space_logsum.reshape(HEADS, S), time_log,
    )
    local = (1, 1, S, D)
    return tuple(result.reshape(local) for result in results[:6]) + tuple(results[6:])


def solution(mesh):
    block = P("clip", "seq", None, None)
    return jax.shard_map(
        shards,
        mesh=mesh,
        in_specs=(block,) * 11 + (P("seq", None),) * 2,
        out_specs=(block,) * 6 + (P("seq", "clip"),) * 2,
        check_vma=False,
    )
```

```python
import math

import jax
import jax.numpy as jnp
from jax import lax
from jax.experimental import pallas as pl
from jax.experimental.pallas import tpu as pltpu
from jax.sharding import PartitionSpec as P

BF16 = jnp.bfloat16
F32 = jnp.float32
HEADS = 16
HEAD = 72
D = HEADS * HEAD
S = 256
SEQ = 16
POS = S // SEQ
CHIPS = 8
YS = 4
ZHS = 4
CHIP_ROWS = 2 * HEAD
YROWS = ZHS * HEAD
WIDE = 384
ZROWS = 80
GROUPS = ((0, 6), (6, 11), (11, 16))
FORWARD = ((0, 512), (512, 896), (896, 1152))
BACK = ((0, 384), (384, 768), (768, 1152))
NT = (((1,), (1,)), ((), ()))
TN = (((0,), (0,)), ((), ()))
NN = (((1,), (0,)), ((), ()))


def mm(a, b, dims):
    return lax.dot_general(a, b, dims, preferred_element_type=F32)


def kernel(
    up, tq, tk, tv, so, to, sq, sk, sv, ws, wt, slog, tlog,
    osq, osk, osv, otq, otk, otv, ows, owt,
    X, R, O, SI, GT, GS, TD, TE, W, wown, w32, w32r,
    ind, bias, cen, cenr, cent, cens,
    ut, utp, mine, psend, prec, ysend, yfar, yrecv, xzsend, xzrecv, zs, zr,
    ld, own_sem, wp_s, wp_r, w1_s, w1_r, lf_s, lf_r, w2_s, w2_r, wf_s, wf_r, w3_s, w3_r, l3_s, l3_r,
    a_s, a_r, c_s, c_r, b_s, b_r, pp_s, pp_r, yf_s, yf_r, y_s, y_r, xz_s, xz_r, z_s, z_r, out_sem,
):
    clip = lax.axis_index("clip")
    seq = lax.axis_index("seq")
    y = lax.rem(clip, YS)
    zh = lax.div(clip, YS)
    core = lax.rem(seq, 2)
    chip = lax.div(seq, 2)
    sibling = seq + 1 - 2 * core
    corner = zh * 2 + core

    def seq_peer(k):
        return lax.rem(seq + k, SEQ)

    def chip_peer(k):
        return 2 * lax.rem(chip + k, CHIPS) + core

    def y_peer(k):
        return zh * YS + lax.rem(y + k, YS)

    def z_peer(k):
        other = lax.rem(corner + k, 2 * ZHS)
        return lax.div(other, 2), lax.rem(other, 2)

    def remote(src, dst, send, recv, **where):
        return pltpu.make_async_remote_copy(
            src_ref=src, dst_ref=dst, send_sem=send, recv_sem=recv,
            device_id=where, device_id_type=pl.DeviceIdType.MESH,
        )

    def drain(ref, sem):
        pltpu.make_async_copy(ref, ref, sem).wait()

    barrier = pltpu.get_barrier_semaphore()
    for k in range(1, SEQ):
        pl.semaphore_signal(barrier, inc=1, device_id={"seq": seq_peer(k)}, device_id_type=pl.DeviceIdType.MESH)
    for k in (1, YS - 1):
        pl.semaphore_signal(barrier, inc=1, device_id={"clip": y_peer(k)}, device_id_type=pl.DeviceIdType.MESH)
    for k in range(1, 2 * ZHS):
        to_zh, to_core = z_peer(k)
        pl.semaphore_signal(
            barrier, inc=1, device_id={"clip": to_zh * YS + y, "seq": 2 * chip + to_core},
            device_id_type=pl.DeviceIdType.MESH,
        )

    loads = [
        pltpu.make_async_copy(src, dst, ld.at[n])
        for n, (src, dst) in enumerate((
            (up, X.at[0]), (tq, X.at[1]), (tk, X.at[2]), (tv, X.at[3]), (so, O.at[0]), (to, O.at[1]),
            (sq, SI.at[0]), (sk, SI.at[1]), (sv, SI.at[2]),
        ))
    ]
    for load in loads:
        load.start()
    w32[0] = wt[...].astype(F32)
    w32[1] = ws[...].astype(F32)

    head_row = lax.broadcasted_iota(jnp.int32, (128, D), 0) * HEAD
    column = lax.broadcasted_iota(jnp.int32, (128, D), 1)
    ind[...] = jnp.where((column >= head_row) & (column < head_row + HEAD), 1.0, 0.0).astype(BF16)
    zeros = jnp.zeros((S, D), BF16)
    for n in range(3):
        TD[n] = zeros
    for ref in (osq, osk, osv):
        ref[...] = zeros
    position = lax.broadcasted_iota(jnp.int32, (S, S), 0)
    other = lax.broadcasted_iota(jnp.int32, (S, S), 1)
    bias[...] = jnp.where(lax.rem(position, POS) == lax.rem(other, POS), 0.0, -1e30)

    pl.semaphore_wait(barrier, (SEQ - 1) + 2 + (2 * ZHS - 1))

    pair = remote(w32, w32r, wp_s, wp_r, seq=sibling)
    pair.start()

    loads[0].wait()
    row_me = pl.ds(pl.multiple_of(seq * POS, POS), POS)

    def rows_of(d):
        return pl.ds(pl.multiple_of(d * POS, POS), POS)

    def send_up(k, carry):
        d = seq_peer(k)
        remote(X.at[0, rows_of(d)], R.at[0, row_me], a_s.at[0], a_r.at[0], seq=d).start()
        return carry

    own_up = pltpu.make_async_copy(X.at[0, row_me], R.at[0, row_me], own_sem.at[0])
    own_up.start()
    for n in range(D // 128):
        ut[128 * n:128 * (n + 1), :] = X[0, :, 128 * n:128 * (n + 1)].astype(F32).T
    pair.wait()
    chip_rows = pl.ds(pl.multiple_of(chip * CHIP_ROWS, 16), CHIP_ROWS)
    tile = pl.ds(pl.multiple_of((2 * y + core) * 128, 128), 128)
    last = pl.ds(D - 128, 128)
    for m in range(2):
        first, second = w32[m], w32r[m]
        low = jnp.where(core == 0, first, second)
        high = jnp.where(core == 0, second, first)
        wown[m] = jnp.concatenate((low, high), axis=0).astype(BF16)
    def stage1(m):
        W[m, chip_rows, tile] = wown[m, :, tile]

        def one(k, carry):
            remote(wown.at[m, :, tile], W.at[m, chip_rows, tile], w1_s.at[m], w1_r.at[m], seq=chip_peer(k)).start()
            return carry

        lax.fori_loop(1, CHIPS, one, 0)

    stage1(0)
    W[core, chip_rows, last] = wown[core, :, last]

    def send_last(k, carry):
        remote(wown.at[core, :, last], W.at[core, chip_rows, last], lf_s, lf_r, seq=chip_peer(k)).start()
        return carry

    lax.fori_loop(1, CHIPS, send_last, 0)
    lax.fori_loop(1, SEQ, send_up, 0)

    for j in range(YS):
        utp[j] = jnp.concatenate(
            [ut[HEAD * (YS * i + j):HEAD * (YS * i + j + 1), :] for i in range(ZHS)], axis=0
        ).astype(BF16)
    loads[4].wait()
    loads[5].wait()
    factor = 1.0 / math.sqrt(lax.axis_size("clip") * SEQ * S)

    def gradient(k):
        rows = utp[lax.rem(y + k, YS)]

        def piece(n, carry):
            columns = pl.ds(pl.multiple_of(n * WIDE, 128), WIDE)
            psend[k, :, columns] = (mm(rows, O[1 - core, :, columns], NN) * factor).astype(BF16)
            mine[k, :, columns] = mm(rows, O[core, :, columns], NN) * factor
            return carry

        lax.fori_loop(0, D // WIDE, piece, 0)
        remote(psend.at[k], prec.at[k], pp_s.at[k], pp_r.at[k], seq=sibling).start()

    def tile_of(k):
        return pl.ds(pl.multiple_of((2 * lax.rem(y + k, YS) + core) * 128, 128), 128)

    def to_sibling(m, k):
        remote(W.at[m, :, tile_of(k)], W.at[m, :, tile_of(k)], w3_s.at[m], w3_r.at[m], seq=sibling).start()

    def stage2(m):
        drain(W.at[m, 0:(CHIPS - 1) * CHIP_ROWS, 0:128], w1_r.at[m])
        for n, k in enumerate((1, YS - 1)):
            remote(W.at[m, :, tile], W.at[m, :, tile], w2_s.at[m], w2_r.at[m, n], clip=y_peer(k)).start()
        to_sibling(m, 0)

    def forward2(m):
        for n, k in enumerate((1, YS - 1)):
            drain(W.at[m, :, 0:128], w2_r.at[m, n])
            half = pl.ds(n * (D // 2), D // 2)
            remote(
                W.at[m, half, tile_of(YS - k)], W.at[m, half, tile_of(YS - k)], wf_s.at[m], wf_r.at[m], clip=y_peer(k)
            ).start()
            to_sibling(m, YS - k)

    def stage3(m):
        drain(W.at[m, :, 0:128], wf_r.at[m])
        to_sibling(m, 2)
        drain(W.at[m, :, 0:512], w3_r.at[m])

    near = ((0, 1, 0, YROWS // 2), (1, YS - 1, YROWS // 2, YROWS))

    def far_chunk():
        drain(prec.at[2], pp_r.at[2])
        ysend[1] = (mine[2] + prec[2].astype(F32)).astype(BF16)
        for n, k, low, top in near:
            remote(ysend.at[1, low:top], yfar.at[n], yf_s.at[n], yf_r.at[n], clip=y_peer(k)).start()

    def near_first():
        for n, k, low, top in near:
            rows = slice(YROWS // 2 - low, YROWS // 2 - low + YROWS // 2)
            drain(prec.at[k], pp_r.at[k])
            ysend[k - 1, rows] = (mine[k, rows] + prec[k, rows].astype(F32)).astype(BF16)
            remote(
                ysend.at[k - 1, rows], yrecv.at[n, rows], y_s.at[0, n], y_r.at[0, n], clip=y_peer(k)
            ).start()

    def near_second():
        for n, k, low, top in near:
            rows = slice(low, top)
            drain(yfar.at[n], yf_r.at[n])
            ysend[k - 1, rows] = (
                mine[k, rows] + prec[k, rows].astype(F32) + yfar[n].astype(F32)
            ).astype(BF16)
            remote(
                ysend.at[k - 1, rows], yrecv.at[n, rows], y_s.at[1, n], y_r.at[1, n], clip=y_peer(k)
            ).start()

    gradient(2)
    stage2(0)
    drain(W.at[0, 0:(CHIPS - 1) * CHIP_ROWS, 0:128], lf_r)
    remote(W.at[core, :, last], W.at[core, :, last], l3_s, l3_r, seq=sibling).start()
    for n in (1, 2, 3):
        loads[n].wait()
    for g, (begin, end) in enumerate(FORWARD):
        columns = pl.ds(begin, end - begin)

        def send_group(k, carry, g=g, columns=columns):
            d = seq_peer(k)
            remote(
                X.at[1:4, rows_of(d), columns], R.at[1:4, row_me, columns], a_s.at[1 + g], a_r.at[1 + g], seq=d
            ).start()
            return carry

        lax.fori_loop(1, SEQ, send_group, 0)
    own_rest = pltpu.make_async_copy(X.at[1:4, row_me], R.at[1:4, row_me], own_sem.at[1])
    own_rest.start()

    gradient(1)
    far_chunk()
    forward2(0)
    stage1(1)
    gradient(3)
    near_first()
    gradient(0)

    stage3(0)
    drain(W.at[0, :, last], l3_r)

    def project(tokens, m, n):
        return mm(tokens, W[m, n * WIDE:(n + 1) * WIDE, :], NT).astype(BF16)

    def split(grad, outputs):
        product = grad.astype(F32) * outputs.astype(F32)
        high = product.astype(BF16)
        return high, (product - high.astype(F32)).astype(BF16)

    total = jnp.zeros((S, 128), F32)
    for n in range(D // WIDE):
        columns = slice(n * WIDE, (n + 1) * WIDE)
        high, low = split(project(X[0], 0, n), O[1, :, columns])
        total = total + (mm(high, ind[:, columns], NT) + mm(low, ind[:, columns], NT))
    cen[...] = total

    def send_center(k, carry):
        d = seq_peer(k)
        remote(cen.at[rows_of(d)], cenr.at[row_me], c_s, c_r, seq=d).start()
        return carry

    lax.fori_loop(1, SEQ, send_center, 0)
    own_cen = pltpu.make_async_copy(cen.at[row_me], cenr.at[row_me], own_sem.at[2])
    own_cen.start()

    near_second()
    others = (SEQ - 1) * POS
    own_up.wait()
    drain(R.at[0, 0:others], a_r.at[0])
    for n in range(D // WIDE):
        GT[:, n * WIDE:(n + 1) * WIDE] = project(R[0], 0, n)
    own_cen.wait()
    drain(cenr.at[0:others], c_r)
    cent[...] = cenr[...].T

    scale = 1.0 / math.sqrt(HEAD)
    lane = lax.broadcasted_iota(jnp.int32, (16, 256), 1)

    def heads(first, end, q_ref, k_ref, v_ref, g_ref, log_ref, center_ref, masked, out):
        def one(h, carry):
            offset = jnp.minimum(lax.div(h * HEAD, 128), D // 128 - 2) * 128
            window = pl.ds(pl.multiple_of(offset, 128), 256)
            begin = h * HEAD - offset
            keep = jnp.where((lane >= begin) & (lane < begin + HEAD), 1.0, 0.0).astype(BF16)
            keep = jnp.broadcast_to(keep[None], (S // 16, 16, 256)).reshape(S, 256)
            q = q_ref[:, window] * keep
            g = g_ref[:, window] * keep
            k = k_ref[:, window]
            v = v_ref[:, window]
            scores = mm(k, q, NT) * scale - log_ref[pl.ds(h, 1), :]
            if masked:
                scores = scores + bias[...]
            probs = jnp.exp(scores)
            dscore = (probs * (mm(v, g, NT) - center_ref[pl.ds(h, 1), :]) * scale).astype(BF16)
            out[0][:, window] = out[0][:, window] + mm(dscore, k * keep, TN).astype(BF16)
            out[1][:, window] = out[1][:, window] + mm(dscore, q, NN).astype(BF16)
            out[2][:, window] = out[2][:, window] + mm(probs.astype(BF16), g, NN).astype(BF16)
            return carry

        lax.fori_loop(first, end, one, 0)

    def over_chips():
        drain(prec.at[0], pp_r.at[0])
        for n in range(2):
            for half in range(2):
                drain(yrecv.at[n, 0:YROWS // 2], y_r.at[half, n])
        for n in range(D // 128):
            columns = slice(128 * n, 128 * (n + 1))
            held = mine[0, :, columns] + prec[0, :, columns].astype(F32)
            for n_from in range(2):
                held = held + yrecv[n_from, :, columns].astype(F32)
            held = jnp.concatenate((held, jnp.zeros((WIDE - YROWS, 128), F32)), axis=0)
            xzsend[128 * n:128 * (n + 1), :] = held.T.astype(BF16)
        for k in range(1, CHIPS):
            there = pl.ds(pl.multiple_of(lax.rem(chip + k, CHIPS) * CHIP_ROWS, 16), CHIP_ROWS)
            remote(xzsend.at[there], xzrecv.at[k - 1], xz_s, xz_r, seq=chip_peer(k)).start()

    own_rest.wait()
    own_back = []
    for n, ((first, end), (begin, stop), (low, top)) in enumerate(zip(GROUPS, FORWARD, BACK)):
        drain(R.at[1:4, 0:others, begin:stop], a_r.at[1 + n])
        heads(first, end, R.at[1], R.at[2], R.at[3], GT, tlog, cent, True, [TD.at[m] for m in range(3)])
        columns = pl.ds(low, top - low)

        def send_back(k, carry, n=n, columns=columns):
            d = seq_peer(k)
            remote(TD.at[:, rows_of(d), columns], TE.at[:, row_me, columns], b_s.at[n], b_r.at[n], seq=d).start()
            return carry

        lax.fori_loop(1, SEQ, send_back, 0)
        back = pltpu.make_async_copy(TD.at[:, row_me, columns], TE.at[:, row_me, columns], own_sem.at[3 + n])
        back.start()
        own_back.append(back)
        if n == 0:
            stage2(1)
        elif n == 1:
            over_chips()
            forward2(1)

    stage3(1)
    total = jnp.zeros((128, S), F32)
    for n in range(D // WIDE):
        columns = slice(n * WIDE, (n + 1) * WIDE)
        grad = project(X[0], 1, n)
        GS[:, columns] = grad
        high, low = split(grad, O[0, :, columns])
        total = total + (mm(ind[:, columns], high, NT) + mm(ind[:, columns], low, NT))
    cens[...] = total
    for n in (6, 7, 8):
        loads[n].wait()
    spatial = (SI.at[0], SI.at[1], SI.at[2], GS, slog, cens, False, (osq, osk, osv))
    heads(0, HEADS // 2, *spatial)

    drain(xzrecv, xz_r)
    held = xzsend[chip_rows, :].astype(F32)
    for k in range(CHIPS - 1):
        held = held + xzrecv[k].astype(F32)
    for i in range(ZHS):
        moved = pltpu.roll(held, WIDE - HEAD * i, axis=1) if i else held
        for c in range(2):
            part = jnp.concatenate((moved[HEAD * c:HEAD * (c + 1), 0:128], jnp.zeros((ZROWS - HEAD, 128), F32)), axis=0)
            zs[2 * i + c] = part.astype(BF16)
    slot = core * ZHS + zh
    for k in range(1, 2 * ZHS):
        to_zh, to_core = z_peer(k)
        remote(
            zs.at[2 * to_zh + to_core], zr.at[slot], z_s, z_r, clip=to_zh * YS + y, seq=2 * chip + to_core
        ).start()
    zr[slot] = zs[corner]
    heads(HEADS // 2, HEADS, *spatial)

    writes = []
    for n, (low, top) in enumerate(BACK):
        own_back[n].wait()
        drain(TE.at[:, 0:others, low:top], b_r.at[n])
    for n, ref in enumerate((otq, otk, otv)):
        write = pltpu.make_async_copy(TE.at[n], ref, out_sem.at[n])
        write.start()
        writes.append(write)

    drain(zr.at[0:2 * ZHS - 1], z_r)
    for m, ref in enumerate((ows, owt)):
        four = [zr[ZHS * m + i].astype(F32) for i in range(ZHS)]
        ref[...] = (four[0] + four[1] + four[2] + four[3])[0:HEAD, 0:HEAD]

    drain(X.at[0, 0:others], a_s.at[0])
    for n, (begin, stop) in enumerate(FORWARD):
        drain(X.at[1:4, 0:others, begin:stop], a_s.at[1 + n])
    for n, (low, top) in enumerate(BACK):
        drain(TD.at[:, 0:others, low:top], b_s.at[n])
    for m in range(2):
        drain(W.at[m, 0:(CHIPS - 1) * CHIP_ROWS, 0:128], w1_s.at[m])
        drain(W.at[m, :, 0:256], w2_s.at[m])
        drain(W.at[m, :, 0:128], wf_s.at[m])
        drain(W.at[m, :, 0:512], w3_s.at[m])
    drain(W.at[0, 0:(CHIPS - 1) * CHIP_ROWS, 0:128], lf_s)
    drain(W.at[0, :, 0:128], l3_s)
    drain(cen.at[0:others], c_s)
    for k in range(YS):
        drain(psend.at[k], pp_s.at[k])
    for n in range(2):
        drain(yfar.at[n], yf_s.at[n])
        for half in range(2):
            drain(yfar.at[n], y_s.at[half, n])
    drain(xzsend.at[0:(CHIPS - 1) * CHIP_ROWS], xz_s)
    drain(zs.at[0:2 * ZHS - 1], z_s)
    for write in writes:
        write.wait()


def write_out(*refs):
    count = len(refs) // 2 - 2
    sources, targets, sem = refs[:count + 2], refs[count + 2:-1], refs[-1]
    copies = [
        pltpu.make_async_copy(src, dst, sem.at[n])
        for n, (src, dst) in enumerate(zip(sources[:count], targets[:count]))
    ]
    for copy in copies:
        copy.start()
    for src, dst in zip(sources[count:], targets[count:]):
        dst[...] = src[...]
    for copy in copies:
        copy.wait()


def shards(
    space_query, space_keys, space_values, space_output, space_logsum,
    time_query, time_keys, time_values, time_output, time_logsum,
    upstream, space_weight, time_weight,
):
    flat = (S, D)
    time_log = time_logsum.reshape(POS, HEADS, SEQ).transpose(1, 2, 0).reshape(HEADS, S)
    dma = pltpu.SemaphoreType.DMA
    big = jax.ShapeDtypeStruct(flat, BF16)
    small = jax.ShapeDtypeStruct((HEAD, HEAD), F32)
    anywhere = pl.BlockSpec(memory_space=pl.ANY)
    held = pl.BlockSpec(memory_space=pltpu.VMEM)
    results = pl.pallas_call(
        kernel,
        out_shape=(pltpu.VMEM(flat, BF16),) * 6 + (pltpu.VMEM((HEAD, HEAD), F32),) * 2,
        in_specs=[anywhere] * 9 + [held] * 4,
        scratch_shapes=[
            pltpu.VMEM((4, S, D), BF16),
            pltpu.VMEM((4, S, D), BF16),
            pltpu.VMEM((2, S, D), BF16),
            pltpu.VMEM((3, S, D), BF16),
            pltpu.VMEM((S, D), BF16),
            pltpu.VMEM((S, D), BF16),
            pltpu.VMEM((3, S, D), BF16),
            pltpu.VMEM((3, S, D), BF16),
            pltpu.VMEM((2, D, D), BF16),
            pltpu.VMEM((2, CHIP_ROWS, D), BF16),
            pltpu.VMEM((2, HEAD, D), F32),
            pltpu.VMEM((2, HEAD, D), F32),
            pltpu.VMEM((128, D), BF16),
            pltpu.VMEM((S, S), F32),
            pltpu.VMEM((S, 128), F32),
            pltpu.VMEM((S, 128), F32),
            pltpu.VMEM((128, S), F32),
            pltpu.VMEM((128, S), F32),
            pltpu.VMEM((D, S), F32),
            pltpu.VMEM((YS, YROWS, S), BF16),
            pltpu.VMEM((YS, YROWS, D), F32),
            pltpu.VMEM((YS, YROWS, D), BF16),
            pltpu.VMEM((YS, YROWS, D), BF16),
            pltpu.VMEM((YS - 1, YROWS, D), BF16),
            pltpu.VMEM((2, YROWS // 2, D), BF16),
            pltpu.VMEM((2, YROWS, D), BF16),
            pltpu.VMEM((D, WIDE), BF16),
            pltpu.VMEM((CHIPS - 1, CHIP_ROWS, WIDE), BF16),
            pltpu.VMEM((2 * ZHS, ZROWS, 128), BF16),
            pltpu.VMEM((2 * ZHS, ZROWS, 128), BF16),
            dma((9,)), dma((6,)), dma, dma, dma((2,)), dma((2,)), dma, dma,
            dma((2,)), dma((2, 2)), dma((2,)), dma((2,)), dma((2,)), dma((2,)), dma, dma,
            dma((4,)), dma((4,)), dma, dma, dma((3,)), dma((3,)), dma((4,)), dma((4,)),
            dma((2,)), dma((2,)), dma((2, 2)), dma((2, 2)), dma, dma, dma, dma, dma((3,)),
        ],
        compiler_params=pltpu.CompilerParams(
            collective_id=0, has_side_effects=True, vmem_limit_bytes=60 * 1024 * 1024 - 256 * 1024
        ),
        cost_estimate=pl.CostEstimate(flops=7_000_000_000, bytes_accessed=12_000_000, transcendentals=2_100_000),
    )(
        upstream.reshape(flat), time_query.reshape(flat), time_keys.reshape(flat), time_values.reshape(flat),
        space_output.reshape(flat), time_output.reshape(flat),
        space_query.reshape(flat), space_keys.reshape(flat), space_values.reshape(flat),
        space_weight, time_weight, space_logsum.reshape(HEADS, S), time_log,
    )
    results = pl.pallas_call(
        write_out,
        out_shape=(big,) * 6 + (small,) * 2,
        in_specs=[anywhere] * 6 + [held] * 2,
        out_specs=(anywhere,) * 6 + (held,) * 2,
        scratch_shapes=[dma((6,))],
        compiler_params=pltpu.CompilerParams(vmem_limit_bytes=1024 * 1024),
    )(*results)
    local = (1, 1, S, D)
    return tuple(result.reshape(local) for result in results[:6]) + tuple(results[6:])


def solution(mesh):
    block = P("clip", "seq", None, None)
    return jax.shard_map(
        shards,
        mesh=mesh,
        in_specs=(block,) * 11 + (P("seq", None),) * 2,
        out_specs=(block,) * 6 + (P("seq", "clip"),) * 2,
        check_vma=False,
    )
```

```python
import math

import jax
import jax.numpy as jnp
from jax import lax
from jax.experimental import pallas as pl
from jax.experimental.pallas import tpu as pltpu
from jax.sharding import PartitionSpec as P

BF16 = jnp.bfloat16
F32 = jnp.float32
HEADS = 16
HEAD = 72
D = HEADS * HEAD
S = 256
SEQ = 16
POS = S // SEQ
CHIPS = 8
YS = 4
ZHS = 4
CHIP_ROWS = 2 * HEAD
YROWS = ZHS * HEAD
WIDE = 384
ZROWS = 80
REST = CHIP_ROWS // 3
GROUPS = ((0, 6), (6, 11), (11, 16))
FORWARD = ((0, 512), (512, 896), (896, 1152))
BACK = ((0, 384), (384, 768), (768, 1152))
NT = (((1,), (1,)), ((), ()))
TN = (((0,), (0,)), ((), ()))
NN = (((1,), (0,)), ((), ()))


def mm(a, b, dims):
    return lax.dot_general(a, b, dims, preferred_element_type=F32)


def kernel(
    up, tq, tk, tv, so, to, sq, sk, sv, ws, wt, slog, tlog,
    osq, osk, osv, otq, otk, otv, ows, owt,
    X, R, O, SI, GT, GS, TD, TE, W, wown, w32, w32r,
    ind, bias, tl, cen, cenr, cent, cens,
    ut, utp, mine, psend, prec, ysend, yfar, yrecv, xzsend, xzrecv, rest, restrecv, zs, zr,
    ld, own_sem, wp_s, wp_r, w1_s, w1_r, lf_s, lf_r, w2_s, w2_r, wf_s, wf_r, w3_s, w3_r, l3_s, l3_r,
    a_s, a_r, c_s, c_r, b_s, b_r, pp_s, pp_r, yf_s, yf_r, y_s, y_r, xz_s, xz_r, xr_s, xr_r, z_s, z_r, out_sem,
):
    clip = lax.axis_index("clip")
    seq = lax.axis_index("seq")
    y = lax.rem(clip, YS)
    zh = lax.div(clip, YS)
    core = lax.rem(seq, 2)
    chip = lax.div(seq, 2)
    sibling = seq + 1 - 2 * core
    corner = zh * 2 + core

    def seq_peer(k):
        return lax.rem(seq + k, SEQ)

    def chip_peer(k):
        return 2 * lax.rem(chip + k, CHIPS) + core

    def y_peer(k):
        return zh * YS + lax.rem(y + k, YS)

    def z_peer(k):
        other = lax.rem(corner + k, 2 * ZHS)
        return lax.div(other, 2), lax.rem(other, 2)

    def remote(src, dst, send, recv, **where):
        return pltpu.make_async_remote_copy(
            src_ref=src, dst_ref=dst, send_sem=send, recv_sem=recv,
            device_id=where, device_id_type=pl.DeviceIdType.MESH,
        )

    def drain(ref, sem):
        pltpu.make_async_copy(ref, ref, sem).wait()

    barrier = pltpu.get_barrier_semaphore()
    for k in range(1, SEQ):
        pl.semaphore_signal(barrier, inc=1, device_id={"seq": seq_peer(k)}, device_id_type=pl.DeviceIdType.MESH)
    for k in (1, YS - 1):
        pl.semaphore_signal(barrier, inc=1, device_id={"clip": y_peer(k)}, device_id_type=pl.DeviceIdType.MESH)
    for k in range(1, 2 * ZHS):
        to_zh, to_core = z_peer(k)
        pl.semaphore_signal(
            barrier, inc=1, device_id={"clip": to_zh * YS + y, "seq": 2 * chip + to_core},
            device_id_type=pl.DeviceIdType.MESH,
        )

    loads = [
        pltpu.make_async_copy(src, dst, ld.at[n])
        for n, (src, dst) in enumerate((
            (up, X.at[0]), (tq, X.at[1]), (tk, X.at[2]), (tv, X.at[3]), (so, O.at[0]), (to, O.at[1]),
            (sq, SI.at[0]), (sk, SI.at[1]), (sv, SI.at[2]),
        ))
    ]
    for load in loads:
        load.start()
    w32[0] = wt[...].astype(F32)
    w32[1] = ws[...].astype(F32)

    pl.semaphore_wait(barrier, (SEQ - 1) + 2 + (2 * ZHS - 1))

    pair = remote(w32, w32r, wp_s, wp_r, seq=sibling)
    pair.start()

    loads[0].wait()
    row_me = pl.ds(pl.multiple_of(seq * POS, POS), POS)

    def rows_of(d):
        return pl.ds(pl.multiple_of(d * POS, POS), POS)

    def send_up(k, carry):
        d = seq_peer(k)
        remote(X.at[0, rows_of(d)], R.at[0, row_me], a_s.at[0], a_r.at[0], seq=d).start()
        return carry

    lax.fori_loop(1, SEQ, send_up, 0)
    own_up = pltpu.make_async_copy(X.at[0, row_me], R.at[0, row_me], own_sem.at[0])
    own_up.start()
    for n in range(D // 128):
        ut[128 * n:128 * (n + 1), :] = X[0, :, 128 * n:128 * (n + 1)].astype(F32).T
    pair.wait()
    chip_rows = pl.ds(pl.multiple_of(chip * CHIP_ROWS, 16), CHIP_ROWS)
    tile = pl.ds(pl.multiple_of((2 * y + core) * 128, 128), 128)
    last = pl.ds(D - 128, 128)
    for m in range(2):
        first, second = w32[m], w32r[m]
        low = jnp.where(core == 0, first, second)
        high = jnp.where(core == 0, second, first)
        wown[m] = jnp.concatenate((low, high), axis=0).astype(BF16)
    def stage1(m):
        W[m, chip_rows, tile] = wown[m, :, tile]

        def one(k, carry):
            remote(wown.at[m, :, tile], W.at[m, chip_rows, tile], w1_s.at[m], w1_r.at[m], seq=chip_peer(k)).start()
            return carry

        lax.fori_loop(1, CHIPS, one, 0)

    stage1(0)
    W[core, chip_rows, last] = wown[core, :, last]

    def send_last(k, carry):
        remote(wown.at[core, :, last], W.at[core, chip_rows, last], lf_s, lf_r, seq=chip_peer(k)).start()
        return carry

    lax.fori_loop(1, CHIPS, send_last, 0)

    head_row = lax.broadcasted_iota(jnp.int32, (128, D), 0) * HEAD
    column = lax.broadcasted_iota(jnp.int32, (128, D), 1)
    ind[...] = jnp.where((column >= head_row) & (column < head_row + HEAD), 1.0, 0.0).astype(BF16)
    zeros = jnp.zeros((S, D), BF16)
    for n in range(3):
        TD[n] = zeros
    for ref in (osq, osk, osv):
        ref[...] = zeros
    position = lax.broadcasted_iota(jnp.int32, (S, S), 0)
    other = lax.broadcasted_iota(jnp.int32, (S, S), 1)
    bias[...] = jnp.where(lax.rem(position, POS) == lax.rem(other, POS), 0.0, -1e30)

    frame = lax.broadcasted_iota(jnp.int32, (SEQ, S), 0) * POS
    place = lax.broadcasted_iota(jnp.int32, (SEQ, S), 1)
    spread = jnp.zeros((HEADS, S), F32)
    for p in range(POS):
        spread = spread + lax.dot_general(
            tlog[p], jnp.where(place == frame + p, 1.0, 0.0), NN,
            precision=lax.Precision.HIGHEST, preferred_element_type=F32,
        )
    tl[...] = spread

    for j in range(YS):
        utp[j] = jnp.concatenate(
            [ut[HEAD * (YS * i + j):HEAD * (YS * i + j + 1), :] for i in range(ZHS)], axis=0
        ).astype(BF16)
    loads[4].wait()
    loads[5].wait()
    factor = 1.0 / math.sqrt(lax.axis_size("clip") * SEQ * S)

    def gradient(k):
        rows = utp[lax.rem(y + k, YS)]

        def piece(n, carry):
            columns = pl.ds(pl.multiple_of(n * WIDE, 128), WIDE)
            psend[k, :, columns] = (mm(rows, O[1 - core, :, columns], NN) * factor).astype(BF16)
            mine[k, :, columns] = mm(rows, O[core, :, columns], NN) * factor
            return carry

        lax.fori_loop(0, D // WIDE, piece, 0)
        remote(psend.at[k], prec.at[k], pp_s.at[k], pp_r.at[k], seq=sibling).start()

    def tile_of(k):
        return pl.ds(pl.multiple_of((2 * lax.rem(y + k, YS) + core) * 128, 128), 128)

    def to_sibling(m, k):
        remote(W.at[m, :, tile_of(k)], W.at[m, :, tile_of(k)], w3_s.at[m], w3_r.at[m], seq=sibling).start()

    def stage2(m):
        drain(W.at[m, 0:(CHIPS - 1) * CHIP_ROWS, 0:128], w1_r.at[m])
        for n, k in enumerate((1, YS - 1)):
            remote(W.at[m, :, tile], W.at[m, :, tile], w2_s.at[m], w2_r.at[m, n], clip=y_peer(k)).start()
        to_sibling(m, 0)

    def forward2(m):
        for n, k in enumerate((1, YS - 1)):
            drain(W.at[m, :, 0:128], w2_r.at[m, n])
            half = pl.ds(n * (D // 2), D // 2)
            remote(
                W.at[m, half, tile_of(YS - k)], W.at[m, half, tile_of(YS - k)], wf_s.at[m], wf_r.at[m], clip=y_peer(k)
            ).start()
            to_sibling(m, YS - k)

    def stage3(m):
        drain(W.at[m, :, 0:128], wf_r.at[m])
        to_sibling(m, 2)
        drain(W.at[m, :, 0:512], w3_r.at[m])

    near = ((0, 1, 0, YROWS // 2), (1, YS - 1, YROWS // 2, YROWS))

    def far_chunk():
        drain(prec.at[2], pp_r.at[2])
        ysend[1] = (mine[2] + prec[2].astype(F32)).astype(BF16)
        for n, k, low, top in near:
            remote(ysend.at[1, low:top], yfar.at[n], yf_s.at[n], yf_r.at[n], clip=y_peer(k)).start()

    def near_first():
        for n, k, low, top in near:
            rows = slice(YROWS // 2 - low, YROWS // 2 - low + YROWS // 2)
            drain(prec.at[k], pp_r.at[k])
            ysend[k - 1, rows] = (mine[k, rows] + prec[k, rows].astype(F32)).astype(BF16)
            remote(
                ysend.at[k - 1, rows], yrecv.at[n, rows], y_s.at[0, n], y_r.at[0, n], clip=y_peer(k)
            ).start()

    def near_second():
        for n, k, low, top in near:
            rows = slice(low, top)
            drain(yfar.at[n], yf_r.at[n])
            ysend[k - 1, rows] = (
                mine[k, rows] + prec[k, rows].astype(F32) + yfar[n].astype(F32)
            ).astype(BF16)
            remote(
                ysend.at[k - 1, rows], yrecv.at[n, rows], y_s.at[1, n], y_r.at[1, n], clip=y_peer(k)
            ).start()

    def forward(g):
        begin, end = FORWARD[g]
        columns = pl.ds(begin, end - begin)

        def send_group(k, carry):
            d = seq_peer(k)
            remote(
                X.at[1:4, rows_of(d), columns], R.at[1:4, row_me, columns], a_s.at[1 + g], a_r.at[1 + g], seq=d
            ).start()
            return carry

        lax.fori_loop(1, SEQ, send_group, 0)

    gradient(2)
    gradient(1)
    far_chunk()
    stage2(0)
    drain(W.at[0, 0:(CHIPS - 1) * CHIP_ROWS, 0:128], lf_r)
    remote(W.at[core, :, last], W.at[core, :, last], l3_s, l3_r, seq=sibling).start()
    for n in (1, 2, 3):
        loads[n].wait()
    forward(0)
    stage1(1)
    forward(1)
    own_rest = pltpu.make_async_copy(X.at[1:4, row_me], R.at[1:4, row_me], own_sem.at[1])
    own_rest.start()
    gradient(3)
    forward2(0)
    near_first()
    near_second()

    stage3(0)
    drain(W.at[0, :, last], l3_r)

    def project(tokens, m, n):
        return mm(tokens, W[m, n * WIDE:(n + 1) * WIDE, :], NT).astype(BF16)

    def split(grad, outputs):
        product = grad.astype(F32) * outputs.astype(F32)
        high = product.astype(BF16)
        return high, (product - high.astype(F32)).astype(BF16)

    total = jnp.zeros((S, 128), F32)
    for n in range(D // WIDE):
        columns = slice(n * WIDE, (n + 1) * WIDE)
        high, low = split(project(X[0], 0, n), O[1, :, columns])
        total = total + (mm(high, ind[:, columns], NT) + mm(low, ind[:, columns], NT))
    high = total.astype(BF16).astype(F32)
    cen[...] = (high + pltpu.roll(total - high, HEADS, axis=1)).astype(BF16)

    def send_center(k, carry):
        d = seq_peer(k)
        remote(cen.at[rows_of(d)], cenr.at[row_me], c_s, c_r, seq=d).start()
        return carry

    lax.fori_loop(1, SEQ, send_center, 0)
    own_cen = pltpu.make_async_copy(cen.at[row_me], cenr.at[row_me], own_sem.at[2])
    own_cen.start()
    forward(2)

    others = (SEQ - 1) * POS
    own_up.wait()
    drain(R.at[0, 0:others], a_r.at[0])
    for n in range(D // WIDE):
        GT[:, n * WIDE:(n + 1) * WIDE] = project(R[0], 0, n)
    gradient(0)
    own_cen.wait()
    drain(cenr.at[0:others], c_r)
    both = cenr[...].astype(F32)
    cent[...] = (both + pltpu.roll(both, 128 - HEADS, axis=1)).T

    scale = 1.0 / math.sqrt(HEAD)
    lane = lax.broadcasted_iota(jnp.int32, (16, 256), 1)

    def heads(first, end, q_ref, k_ref, v_ref, g_ref, log_ref, center_ref, masked, out):
        def one(h, carry):
            offset = jnp.minimum(lax.div(h * HEAD, 128), D // 128 - 2) * 128
            window = pl.ds(pl.multiple_of(offset, 128), 256)
            begin = h * HEAD - offset
            keep = jnp.where((lane >= begin) & (lane < begin + HEAD), 1.0, 0.0).astype(BF16)
            keep = jnp.broadcast_to(keep[None], (S // 16, 16, 256)).reshape(S, 256)
            q = q_ref[:, window] * keep
            g = g_ref[:, window] * keep
            k = k_ref[:, window]
            v = v_ref[:, window]
            scores = mm(k, q, NT) * scale - log_ref[pl.ds(h, 1), :]
            if masked:
                scores = scores + bias[...]
            probs = jnp.exp(scores)
            dscore = (probs * (mm(v, g, NT) - center_ref[pl.ds(h, 1), :]) * scale).astype(BF16)
            out[0][:, window] = out[0][:, window] + mm(dscore, k * keep, TN).astype(BF16)
            out[1][:, window] = out[1][:, window] + mm(dscore, q, NN).astype(BF16)
            out[2][:, window] = out[2][:, window] + mm(probs.astype(BF16), g, NN).astype(BF16)
            return carry

        lax.fori_loop(first, end, one, 0)

    def over_chips():
        drain(prec.at[0], pp_r.at[0])
        for n in range(2):
            for half in range(2):
                drain(yrecv.at[n, 0:YROWS // 2], y_r.at[half, n])
        for n in range(D // 128):
            columns = slice(128 * n, 128 * (n + 1))
            held = mine[0, :, columns] + prec[0, :, columns].astype(F32)
            for n_from in range(2):
                held = held + yrecv[n_from, :, columns].astype(F32)
            held = jnp.concatenate((held, jnp.zeros((WIDE - YROWS, 128), F32)), axis=0)
            xzsend[128 * n:128 * (n + 1), :] = held.T.astype(BF16)
        for c in range(CHIPS):
            parts = [
                xzsend[CHIP_ROWS * c + REST * g:CHIP_ROWS * c + REST * (g + 1), 256:WIDE].astype(F32)
                for g in range(3)
            ]
            rest[REST * c:REST * (c + 1), :] = (
                parts[0] + pltpu.roll(parts[1], 32, axis=1) + pltpu.roll(parts[2], 64, axis=1)
            ).astype(BF16)
        for k in range(1, CHIPS):
            to_chip = lax.rem(chip + k, CHIPS)
            there = pl.ds(pl.multiple_of(to_chip * CHIP_ROWS, 16), CHIP_ROWS)
            remote(xzsend.at[there, 0:256], xzrecv.at[k - 1], xz_s, xz_r, seq=chip_peer(k)).start()
            there = pl.ds(pl.multiple_of(to_chip * REST, 16), REST)
            remote(rest.at[there], restrecv.at[k - 1], xr_s, xr_r, seq=chip_peer(k)).start()

    own_rest.wait()
    own_back = []
    for n, ((first, end), (begin, stop), (low, top)) in enumerate(zip(GROUPS, FORWARD, BACK)):
        drain(R.at[1:4, 0:others, begin:stop], a_r.at[1 + n])
        heads(first, end, R.at[1], R.at[2], R.at[3], GT, tl, cent, True, [TD.at[m] for m in range(3)])
        columns = pl.ds(low, top - low)

        def send_back(k, carry, n=n, columns=columns):
            d = seq_peer(k)
            remote(TD.at[:, rows_of(d), columns], TE.at[:, row_me, columns], b_s.at[n], b_r.at[n], seq=d).start()
            return carry

        lax.fori_loop(1, SEQ, send_back, 0)
        back = pltpu.make_async_copy(TD.at[:, row_me, columns], TE.at[:, row_me, columns], own_sem.at[3 + n])
        back.start()
        own_back.append(back)
        if n == 0:
            over_chips()
            stage2(1)
        elif n == 1:
            forward2(1)

    stage3(1)
    total = jnp.zeros((128, S), F32)
    for n in range(D // WIDE):
        columns = slice(n * WIDE, (n + 1) * WIDE)
        grad = project(X[0], 1, n)
        GS[:, columns] = grad
        high, low = split(grad, O[0, :, columns])
        total = total + (mm(ind[:, columns], high, NT) + mm(ind[:, columns], low, NT))
    cens[...] = total
    for n in (6, 7, 8):
        loads[n].wait()
    spatial = (SI.at[0], SI.at[1], SI.at[2], GS, slog, cens, False, (osq, osk, osv))
    drain(xzrecv, xz_r)
    drain(restrecv, xr_r)
    held = xzsend[chip_rows, 0:256].astype(F32)
    side = rest[pl.ds(pl.multiple_of(chip * REST, 16), REST), :].astype(F32)
    for k in range(CHIPS - 1):
        held = held + xzrecv[k].astype(F32)
        side = side + restrecv[k].astype(F32)
    side = jnp.concatenate((side, pltpu.roll(side, 96, axis=1), pltpu.roll(side, 64, axis=1)), axis=0)
    held = jnp.concatenate((held, side), axis=1)
    for i in range(ZHS):
        moved = pltpu.roll(held, WIDE - HEAD * i, axis=1) if i else held
        for c in range(2):
            part = jnp.concatenate((moved[HEAD * c:HEAD * (c + 1), 0:128], jnp.zeros((ZROWS - HEAD, 128), F32)), axis=0)
            zs[2 * i + c] = part.astype(BF16)
    slot = core * ZHS + zh
    for k in range(1, 2 * ZHS):
        to_zh, to_core = z_peer(k)
        remote(
            zs.at[2 * to_zh + to_core], zr.at[slot], z_s, z_r, clip=to_zh * YS + y, seq=2 * chip + to_core
        ).start()
    zr[slot] = zs[corner]
    heads(0, HEADS, *spatial)


    writes = []
    for n, (low, top) in enumerate(BACK):
        own_back[n].wait()
        drain(TE.at[:, 0:others, low:top], b_r.at[n])
    for n, ref in enumerate((otq, otk, otv)):
        write = pltpu.make_async_copy(TE.at[n], ref, out_sem.at[n])
        write.start()
        writes.append(write)

    drain(zr.at[0:2 * ZHS - 1], z_r)
    for m, ref in enumerate((ows, owt)):
        four = [zr[ZHS * m + i].astype(F32) for i in range(ZHS)]
        ref[...] = (four[0] + four[1] + four[2] + four[3])[0:HEAD, 0:HEAD]

    drain(X.at[0, 0:others], a_s.at[0])
    for n, (begin, stop) in enumerate(FORWARD):
        drain(X.at[1:4, 0:others, begin:stop], a_s.at[1 + n])
    for n, (low, top) in enumerate(BACK):
        drain(TD.at[:, 0:others, low:top], b_s.at[n])
    for m in range(2):
        drain(W.at[m, 0:(CHIPS - 1) * CHIP_ROWS, 0:128], w1_s.at[m])
        drain(W.at[m, :, 0:256], w2_s.at[m])
        drain(W.at[m, :, 0:128], wf_s.at[m])
        drain(W.at[m, :, 0:512], w3_s.at[m])
    drain(W.at[0, 0:(CHIPS - 1) * CHIP_ROWS, 0:128], lf_s)
    drain(W.at[0, :, 0:128], l3_s)
    drain(cen.at[0:others], c_s)
    for k in range(YS):
        drain(psend.at[k], pp_s.at[k])
    for n in range(2):
        drain(yfar.at[n], yf_s.at[n])
        for half in range(2):
            drain(yfar.at[n], y_s.at[half, n])
    drain(xzsend.at[0:(CHIPS - 1) * CHIP_ROWS, 0:256], xz_s)
    drain(rest.at[0:(CHIPS - 1) * REST], xr_s)
    drain(zs.at[0:2 * ZHS - 1], z_s)
    for write in writes:
        write.wait()


def write_out(*refs):
    count = len(refs) // 2 - 2
    sources, targets, sem = refs[:count + 2], refs[count + 2:-1], refs[-1]
    copies = [
        pltpu.make_async_copy(src, dst, sem.at[n])
        for n, (src, dst) in enumerate(zip(sources[:count], targets[:count]))
    ]
    for copy in copies:
        copy.start()
    for src, dst in zip(sources[count:], targets[count:]):
        dst[...] = src[...]
    for copy in copies:
        copy.wait()


def shards(
    space_query, space_keys, space_values, space_output, space_logsum,
    time_query, time_keys, time_values, time_output, time_logsum,
    upstream, space_weight, time_weight,
):
    flat = (S, D)
    dma = pltpu.SemaphoreType.DMA
    big = jax.ShapeDtypeStruct(flat, BF16)
    small = jax.ShapeDtypeStruct((HEAD, HEAD), F32)
    anywhere = pl.BlockSpec(memory_space=pl.ANY)
    held = pl.BlockSpec(memory_space=pltpu.VMEM)
    results = pl.pallas_call(
        kernel,
        out_shape=(pltpu.VMEM(flat, BF16),) * 6 + (pltpu.VMEM((HEAD, HEAD), F32),) * 2,
        in_specs=[anywhere] * 9 + [held] * 4,
        scratch_shapes=[
            pltpu.VMEM((4, S, D), BF16),
            pltpu.VMEM((4, S, D), BF16),
            pltpu.VMEM((2, S, D), BF16),
            pltpu.VMEM((3, S, D), BF16),
            pltpu.VMEM((S, D), BF16),
            pltpu.VMEM((S, D), BF16),
            pltpu.VMEM((3, S, D), BF16),
            pltpu.VMEM((3, S, D), BF16),
            pltpu.VMEM((2, D, D), BF16),
            pltpu.VMEM((2, CHIP_ROWS, D), BF16),
            pltpu.VMEM((2, HEAD, D), F32),
            pltpu.VMEM((2, HEAD, D), F32),
            pltpu.VMEM((128, D), BF16),
            pltpu.VMEM((S, S), F32),
            pltpu.VMEM((HEADS, S), F32),
            pltpu.VMEM((S, 128), BF16),
            pltpu.VMEM((S, 128), BF16),
            pltpu.VMEM((128, S), F32),
            pltpu.VMEM((128, S), F32),
            pltpu.VMEM((D, S), F32),
            pltpu.VMEM((YS, YROWS, S), BF16),
            pltpu.VMEM((YS, YROWS, D), F32),
            pltpu.VMEM((YS, YROWS, D), BF16),
            pltpu.VMEM((YS, YROWS, D), BF16),
            pltpu.VMEM((YS - 1, YROWS, D), BF16),
            pltpu.VMEM((2, YROWS // 2, D), BF16),
            pltpu.VMEM((2, YROWS, D), BF16),
            pltpu.VMEM((D, WIDE), BF16),
            pltpu.VMEM((CHIPS - 1, CHIP_ROWS, 256), BF16),
            pltpu.VMEM((CHIPS * REST, 128), BF16),
            pltpu.VMEM((CHIPS - 1, REST, 128), BF16),
            pltpu.VMEM((2 * ZHS, ZROWS, 128), BF16),
            pltpu.VMEM((2 * ZHS, ZROWS, 128), BF16),
            dma((9,)), dma((6,)), dma, dma, dma((2,)), dma((2,)), dma, dma,
            dma((2,)), dma((2, 2)), dma((2,)), dma((2,)), dma((2,)), dma((2,)), dma, dma,
            dma((4,)), dma((4,)), dma, dma, dma((3,)), dma((3,)), dma((4,)), dma((4,)),
            dma((2,)), dma((2,)), dma((2, 2)), dma((2, 2)), dma, dma, dma, dma, dma, dma, dma((3,)),
        ],
        compiler_params=pltpu.CompilerParams(
            collective_id=0, has_side_effects=True, vmem_limit_bytes=60 * 1024 * 1024 - 256 * 1024
        ),
        cost_estimate=pl.CostEstimate(flops=7_000_000_000, bytes_accessed=12_000_000, transcendentals=2_100_000),
    )(
        upstream.reshape(flat), time_query.reshape(flat), time_keys.reshape(flat), time_values.reshape(flat),
        space_output.reshape(flat), time_output.reshape(flat),
        space_query.reshape(flat), space_keys.reshape(flat), space_values.reshape(flat),
        space_weight, time_weight, space_logsum.reshape(HEADS, S), time_logsum.reshape(POS, HEADS, SEQ),
    )
    results = pl.pallas_call(
        write_out,
        out_shape=(big,) * 6 + (small,) * 2,
        in_specs=[anywhere] * 6 + [held] * 2,
        out_specs=(anywhere,) * 6 + (held,) * 2,
        scratch_shapes=[dma((6,))],
        compiler_params=pltpu.CompilerParams(vmem_limit_bytes=1024 * 1024),
    )(*results)
    local = (1, 1, S, D)
    return tuple(result.reshape(local) for result in results[:6]) + tuple(results[6:])


def solution(mesh):
    block = P("clip", "seq", None, None)
    return jax.shard_map(
        shards,
        mesh=mesh,
        in_specs=(block,) * 11 + (P("seq", None),) * 2,
        out_specs=(block,) * 6 + (P("seq", "clip"),) * 2,
        check_vma=False,
    )
```

```python
import math

import jax
import jax.numpy as jnp
from jax import lax
from jax.experimental import pallas as pl
from jax.experimental.pallas import tpu as pltpu
from jax.sharding import PartitionSpec as P

BF16 = jnp.bfloat16
F32 = jnp.float32
HEADS = 16
HEAD = 72
D = HEADS * HEAD
S = 256
SEQ = 16
POS = S // SEQ
CHIPS = 8
YS = 4
ZHS = 4
CHIP_ROWS = 2 * HEAD
YROWS = ZHS * HEAD
WIDE = 384
ZROWS = 80
PART = 32
REST = CHIP_ROWS // 3
GROUPS = ((0, 6), (6, 11), (11, 16))
FORWARD = ((0, 512), (512, 896), (896, 1152))
BACK = ((0, 384), (384, 768), (768, 1152))
NT = (((1,), (1,)), ((), ()))
TN = (((0,), (0,)), ((), ()))
NN = (((1,), (0,)), ((), ()))


def mm(a, b, dims):
    return lax.dot_general(a, b, dims, preferred_element_type=F32)


def kernel(
    up, tq, tk, tv, so, to, sq, sk, sv, ws, wt, slog, tlog,
    osq, osk, osv, otq, otk, otv, ows, owt,
    X, R, O, SI, GT, GS, TD, TE, W, L, wown, w32, w32r,
    ind, bias, tl, cen, cenr, cent, cens,
    ut, utp, mine, psend, prec, ysend, yfar, yrecv, xzsend, xzrecv, rest, restrecv, zs, zr,
    ld, own_sem, wp_s, wp_r, w1_s, w1_r, lf_s, lf_r, lg_s, lg_r, l2_s, l2_r, l4_s, l4_r, w2_s, w2_r, wf_s, wf_r, w3_s, w3_r, l3_s, l3_r,
    a_s, a_r, c_s, c_r, b_s, b_r, pp_s, pp_r, yf_s, yf_r, y_s, y_r, xz_s, xz_r, xr_s, xr_r, z_s, z_r, out_sem,
):
    clip = lax.axis_index("clip")
    seq = lax.axis_index("seq")
    y = lax.rem(clip, YS)
    zh = lax.div(clip, YS)
    core = lax.rem(seq, 2)
    chip = lax.div(seq, 2)
    sibling = seq + 1 - 2 * core
    corner = zh * 2 + core

    def seq_peer(k):
        return lax.rem(seq + k, SEQ)

    def chip_peer(k):
        return 2 * lax.rem(chip + k, CHIPS) + core

    def y_peer(k):
        return zh * YS + lax.rem(y + k, YS)

    def z_peer(k):
        other = lax.rem(corner + k, 2 * ZHS)
        return lax.div(other, 2), lax.rem(other, 2)

    def remote(src, dst, send, recv, **where):
        return pltpu.make_async_remote_copy(
            src_ref=src, dst_ref=dst, send_sem=send, recv_sem=recv,
            device_id=where, device_id_type=pl.DeviceIdType.MESH,
        )

    def drain(ref, sem):
        pltpu.make_async_copy(ref, ref, sem).wait()

    barrier = pltpu.get_barrier_semaphore()
    for k in range(1, SEQ):
        pl.semaphore_signal(barrier, inc=1, device_id={"seq": seq_peer(k)}, device_id_type=pl.DeviceIdType.MESH)
    for k in (1, YS - 1):
        pl.semaphore_signal(barrier, inc=1, device_id={"clip": y_peer(k)}, device_id_type=pl.DeviceIdType.MESH)
    for k in range(1, 2 * ZHS):
        to_zh, to_core = z_peer(k)
        pl.semaphore_signal(
            barrier, inc=1, device_id={"clip": to_zh * YS + y, "seq": 2 * chip + to_core},
            device_id_type=pl.DeviceIdType.MESH,
        )

    loads = [
        pltpu.make_async_copy(src, dst, ld.at[n])
        for n, (src, dst) in enumerate((
            (up, X.at[0]), (tq, X.at[1]), (tk, X.at[2]), (tv, X.at[3]), (so, O.at[0]), (to, O.at[1]),
            (sq, SI.at[0]), (sk, SI.at[1]), (sv, SI.at[2]),
        ))
    ]
    for load in loads:
        load.start()
    w32[0] = wt[...].astype(F32)
    w32[1] = ws[...].astype(F32)

    pl.semaphore_wait(barrier, (SEQ - 1) + 2 + (2 * ZHS - 1))

    pair = remote(w32, w32r, wp_s, wp_r, seq=sibling)
    pair.start()

    loads[0].wait()
    row_me = pl.ds(pl.multiple_of(seq * POS, POS), POS)

    def rows_of(d):
        return pl.ds(pl.multiple_of(d * POS, POS), POS)

    def send_up(k, carry):
        d = seq_peer(k)
        remote(X.at[0, rows_of(d)], R.at[0, row_me], a_s.at[0], a_r.at[0], seq=d).start()
        return carry

    lax.fori_loop(1, SEQ, send_up, 0)
    own_up = pltpu.make_async_copy(X.at[0, row_me], R.at[0, row_me], own_sem.at[0])
    own_up.start()
    for n in range(D // 128):
        ut[128 * n:128 * (n + 1), :] = X[0, :, 128 * n:128 * (n + 1)].astype(F32).T
    pair.wait()
    chip_rows = pl.ds(pl.multiple_of(chip * CHIP_ROWS, 16), CHIP_ROWS)
    tile = pl.ds(pl.multiple_of((2 * y + core) * 128, 128), 128)
    last = pl.ds(D - 128, 128)
    for m in range(2):
        first, second = w32[m], w32r[m]
        low = jnp.where(core == 0, first, second)
        high = jnp.where(core == 0, second, first)
        wown[m] = jnp.concatenate((low, high), axis=0).astype(BF16)
    def stage1(m):
        W[m, chip_rows, tile] = wown[m, :, tile]

        def one(k, carry):
            remote(wown.at[m, :, tile], W.at[m, chip_rows, tile], w1_s.at[m], w1_r.at[m], seq=chip_peer(k)).start()
            return carry

        lax.fori_loop(1, CHIPS, one, 0)

    stage1(0)
    def part_of(k):
        return pl.ds(pl.multiple_of(lax.rem(y + k, YS) * PART, PART), PART)

    part, end_rows = part_of(0), pl.ds(YS * PART, CHIP_ROWS - YS * PART)
    L[chip, part, :] = wown[core, part, last]
    L[chip, end_rows, :] = wown[core, end_rows, last]

    def send_last(k, carry):
        remote(wown.at[core, part, last], L.at[chip, part], lf_s, lf_r, seq=chip_peer(k)).start()
        remote(wown.at[core, end_rows, last], L.at[chip, end_rows], lg_s, lg_r, seq=chip_peer(k)).start()
        return carry

    lax.fori_loop(1, CHIPS, send_last, 0)

    head_row = lax.broadcasted_iota(jnp.int32, (128, D), 0) * HEAD
    column = lax.broadcasted_iota(jnp.int32, (128, D), 1)
    ind[...] = jnp.where((column >= head_row) & (column < head_row + HEAD), 1.0, 0.0).astype(BF16)
    zeros = jnp.zeros((S, D), BF16)
    for n in range(3):
        TD[n] = zeros
    for ref in (osq, osk, osv):
        ref[...] = zeros
    position = lax.broadcasted_iota(jnp.int32, (S, S), 0)
    other = lax.broadcasted_iota(jnp.int32, (S, S), 1)
    bias[...] = jnp.where(lax.rem(position, POS) == lax.rem(other, POS), 0.0, -1e30)

    frame = lax.broadcasted_iota(jnp.int32, (SEQ, S), 0) * POS
    place = lax.broadcasted_iota(jnp.int32, (SEQ, S), 1)
    spread = jnp.zeros((HEADS, S), F32)
    for p in range(POS):
        spread = spread + lax.dot_general(
            tlog[p], jnp.where(place == frame + p, 1.0, 0.0), NN,
            precision=lax.Precision.HIGHEST, preferred_element_type=F32,
        )
    tl[...] = spread

    for j in range(YS):
        utp[j] = jnp.concatenate(
            [ut[HEAD * (YS * i + j):HEAD * (YS * i + j + 1), :] for i in range(ZHS)], axis=0
        ).astype(BF16)
    loads[4].wait()
    loads[5].wait()
    factor = 1.0 / math.sqrt(lax.axis_size("clip") * SEQ * S)

    def gradient(k):
        rows = utp[lax.rem(y + k, YS)]

        def piece(n, carry):
            columns = pl.ds(pl.multiple_of(n * WIDE, 128), WIDE)
            psend[k, :, columns] = (mm(rows, O[1 - core, :, columns], NN) * factor).astype(BF16)
            mine[k, :, columns] = mm(rows, O[core, :, columns], NN) * factor
            return carry

        lax.fori_loop(0, D // WIDE, piece, 0)
        remote(psend.at[k], prec.at[k], pp_s.at[k], pp_r.at[k], seq=sibling).start()

    def tile_of(k):
        return pl.ds(pl.multiple_of((2 * lax.rem(y + k, YS) + core) * 128, 128), 128)

    def to_sibling(m, k):
        remote(W.at[m, :, tile_of(k)], W.at[m, :, tile_of(k)], w3_s.at[m], w3_r.at[m], seq=sibling).start()

    def stage2(m):
        drain(W.at[m, 0:(CHIPS - 1) * CHIP_ROWS, 0:128], w1_r.at[m])
        for n, k in enumerate((1, YS - 1)):
            remote(W.at[m, :, tile], W.at[m, :, tile], w2_s.at[m], w2_r.at[m, n], clip=y_peer(k)).start()
        to_sibling(m, 0)

    def forward2(m):
        for n, k in enumerate((1, YS - 1)):
            drain(W.at[m, :, 0:128], w2_r.at[m, n])
            half = pl.ds(n * (D // 2), D // 2)
            remote(
                W.at[m, half, tile_of(YS - k)], W.at[m, half, tile_of(YS - k)], wf_s.at[m], wf_r.at[m], clip=y_peer(k)
            ).start()
            to_sibling(m, YS - k)

    def stage3(m):
        drain(W.at[m, :, 0:128], wf_r.at[m])
        to_sibling(m, 2)
        drain(W.at[m, :, 0:512], w3_r.at[m])

    near = ((0, 1, 0, YROWS // 2), (1, YS - 1, YROWS // 2, YROWS))

    def far_chunk():
        drain(prec.at[2], pp_r.at[2])
        ysend[1] = (mine[2] + prec[2].astype(F32)).astype(BF16)
        for n, k, low, top in near:
            remote(ysend.at[1, low:top], yfar.at[n], yf_s.at[n], yf_r.at[n], clip=y_peer(k)).start()

    def near_first():
        for n, k, low, top in near:
            rows = slice(YROWS // 2 - low, YROWS // 2 - low + YROWS // 2)
            drain(prec.at[k], pp_r.at[k])
            ysend[k - 1, rows] = (mine[k, rows] + prec[k, rows].astype(F32)).astype(BF16)
            remote(
                ysend.at[k - 1, rows], yrecv.at[n, rows], y_s.at[0, n], y_r.at[0, n], clip=y_peer(k)
            ).start()

    def near_second():
        for n, k, low, top in near:
            rows = slice(low, top)
            drain(yfar.at[n], yf_r.at[n])
            ysend[k - 1, rows] = (
                mine[k, rows] + prec[k, rows].astype(F32) + yfar[n].astype(F32)
            ).astype(BF16)
            remote(
                ysend.at[k - 1, rows], yrecv.at[n, rows], y_s.at[1, n], y_r.at[1, n], clip=y_peer(k)
            ).start()

    def forward(g):
        begin, end = FORWARD[g]
        columns = pl.ds(begin, end - begin)

        def send_group(k, carry):
            d = seq_peer(k)
            remote(
                X.at[1:4, rows_of(d), columns], R.at[1:4, row_me, columns], a_s.at[1 + g], a_r.at[1 + g], seq=d
            ).start()
            return carry

        lax.fori_loop(1, SEQ, send_group, 0)

    gradient(2)
    gradient(1)
    far_chunk()
    stage2(0)
    drain(L.at[0:CHIPS - 1, 0:PART], lf_r)
    for n, k in enumerate((1, YS - 1)):
        remote(L.at[:, part], L.at[:, part], l2_s, l2_r.at[n], clip=y_peer(k)).start()
    for n in (1, 2, 3):
        loads[n].wait()
    forward(0)
    stage1(1)
    forward(1)
    own_rest = pltpu.make_async_copy(X.at[1:4, row_me], R.at[1:4, row_me], own_sem.at[1])
    own_rest.start()
    gradient(3)
    forward2(0)
    for n, k in enumerate((1, YS - 1)):
        drain(L.at[:, 0:PART], l2_r.at[n])
        there = L.at[pl.ds(n * (CHIPS // 2), CHIPS // 2), part_of(YS - k)]
        remote(there, there, l4_s, l4_r, clip=y_peer(k)).start()
    near_first()
    near_second()
    drain(L.at[:, 0:PART], l4_r)
    drain(L.at[0:CHIPS - 1, 0:CHIP_ROWS - YS * PART], lg_r)
    W[core, :, last] = L[...].reshape(D, 128)
    remote(W.at[core, :, last], W.at[core, :, last], l3_s, l3_r, seq=sibling).start()

    stage3(0)
    drain(W.at[0, :, last], l3_r)

    def project(tokens, m, n):
        return mm(tokens, W[m, n * WIDE:(n + 1) * WIDE, :], NT).astype(BF16)

    def split(grad, outputs):
        product = grad.astype(F32) * outputs.astype(F32)
        high = product.astype(BF16)
        return high, (product - high.astype(F32)).astype(BF16)

    total = jnp.zeros((S, 128), F32)
    for n in range(D // WIDE):
        columns = slice(n * WIDE, (n + 1) * WIDE)
        high, low = split(project(X[0], 0, n), O[1, :, columns])
        total = total + (mm(high, ind[:, columns], NT) + mm(low, ind[:, columns], NT))
    high = total.astype(BF16).astype(F32)
    cen[...] = (high + pltpu.roll(total - high, HEADS, axis=1)).astype(BF16)

    def send_center(k, carry):
        d = seq_peer(k)
        remote(cen.at[rows_of(d)], cenr.at[row_me], c_s, c_r, seq=d).start()
        return carry

    lax.fori_loop(1, SEQ, send_center, 0)
    own_cen = pltpu.make_async_copy(cen.at[row_me], cenr.at[row_me], own_sem.at[2])
    own_cen.start()
    forward(2)

    others = (SEQ - 1) * POS
    own_up.wait()
    drain(R.at[0, 0:others], a_r.at[0])
    for n in range(D // WIDE):
        GT[:, n * WIDE:(n + 1) * WIDE] = project(R[0], 0, n)
    gradient(0)
    own_cen.wait()
    drain(cenr.at[0:others], c_r)
    both = cenr[...].astype(F32)
    cent[...] = (both + pltpu.roll(both, 128 - HEADS, axis=1)).T

    scale = 1.0 / math.sqrt(HEAD)
    lane = lax.broadcasted_iota(jnp.int32, (16, 256), 1)

    def heads(first, end, q_ref, k_ref, v_ref, g_ref, log_ref, center_ref, masked, out):
        def one(h, carry):
            offset = jnp.minimum(lax.div(h * HEAD, 128), D // 128 - 2) * 128
            window = pl.ds(pl.multiple_of(offset, 128), 256)
            begin = h * HEAD - offset
            keep = jnp.where((lane >= begin) & (lane < begin + HEAD), 1.0, 0.0).astype(BF16)
            keep = jnp.broadcast_to(keep[None], (S // 16, 16, 256)).reshape(S, 256)
            q = q_ref[:, window] * keep
            g = g_ref[:, window] * keep
            k = k_ref[:, window]
            v = v_ref[:, window]
            scores = mm(k, q, NT) * scale - log_ref[pl.ds(h, 1), :]
            if masked:
                scores = scores + bias[...]
            probs = jnp.exp(scores)
            dscore = (probs * (mm(v, g, NT) - center_ref[pl.ds(h, 1), :]) * scale).astype(BF16)
            out[0][:, window] = out[0][:, window] + mm(dscore, k * keep, TN).astype(BF16)
            out[1][:, window] = out[1][:, window] + mm(dscore, q, NN).astype(BF16)
            out[2][:, window] = out[2][:, window] + mm(probs.astype(BF16), g, NN).astype(BF16)
            return carry

        lax.fori_loop(first, end, one, 0)

    def over_chips():
        drain(prec.at[0], pp_r.at[0])
        for n in range(2):
            for half in range(2):
                drain(yrecv.at[n, 0:YROWS // 2], y_r.at[half, n])
        for n in range(D // 128):
            columns = slice(128 * n, 128 * (n + 1))
            held = mine[0, :, columns] + prec[0, :, columns].astype(F32)
            for n_from in range(2):
                held = held + yrecv[n_from, :, columns].astype(F32)
            held = jnp.concatenate((held, jnp.zeros((WIDE - YROWS, 128), F32)), axis=0)
            xzsend[128 * n:128 * (n + 1), :] = held.T.astype(BF16)
        for c in range(CHIPS):
            parts = [
                xzsend[CHIP_ROWS * c + REST * g:CHIP_ROWS * c + REST * (g + 1), 256:WIDE].astype(F32)
                for g in range(3)
            ]
            rest[REST * c:REST * (c + 1), :] = (
                parts[0] + pltpu.roll(parts[1], 32, axis=1) + pltpu.roll(parts[2], 64, axis=1)
            ).astype(BF16)
        for k in range(1, CHIPS):
            to_chip = lax.rem(chip + k, CHIPS)
            there = pl.ds(pl.multiple_of(to_chip * CHIP_ROWS, 16), CHIP_ROWS)
            remote(xzsend.at[there, 0:256], xzrecv.at[k - 1], xz_s, xz_r, seq=chip_peer(k)).start()
            there = pl.ds(pl.multiple_of(to_chip * REST, 16), REST)
            remote(rest.at[there], restrecv.at[k - 1], xr_s, xr_r, seq=chip_peer(k)).start()

    own_rest.wait()
    own_back = []
    for n, ((first, end), (begin, stop), (low, top)) in enumerate(zip(GROUPS, FORWARD, BACK)):
        drain(R.at[1:4, 0:others, begin:stop], a_r.at[1 + n])
        heads(first, end, R.at[1], R.at[2], R.at[3], GT, tl, cent, True, [TD.at[m] for m in range(3)])
        columns = pl.ds(low, top - low)

        def send_back(k, carry, n=n, columns=columns):
            d = seq_peer(k)
            remote(TD.at[:, rows_of(d), columns], TE.at[:, row_me, columns], b_s.at[n], b_r.at[n], seq=d).start()
            return carry

        lax.fori_loop(1, SEQ, send_back, 0)
        back = pltpu.make_async_copy(TD.at[:, row_me, columns], TE.at[:, row_me, columns], own_sem.at[3 + n])
        back.start()
        own_back.append(back)
        if n == 0:
            over_chips()
            stage2(1)
        elif n == 1:
            forward2(1)

    stage3(1)
    total = jnp.zeros((128, S), F32)
    for n in range(D // WIDE):
        columns = slice(n * WIDE, (n + 1) * WIDE)
        grad = project(X[0], 1, n)
        GS[:, columns] = grad
        high, low = split(grad, O[0, :, columns])
        total = total + (mm(ind[:, columns], high, NT) + mm(ind[:, columns], low, NT))
    cens[...] = total
    for n in (6, 7, 8):
        loads[n].wait()
    spatial = (SI.at[0], SI.at[1], SI.at[2], GS, slog, cens, False, (osq, osk, osv))
    drain(xzrecv, xz_r)
    drain(restrecv, xr_r)
    held = xzsend[chip_rows, 0:256].astype(F32)
    side = rest[pl.ds(pl.multiple_of(chip * REST, 16), REST), :].astype(F32)
    for k in range(CHIPS - 1):
        held = held + xzrecv[k].astype(F32)
        side = side + restrecv[k].astype(F32)
    side = jnp.concatenate((side, pltpu.roll(side, 96, axis=1), pltpu.roll(side, 64, axis=1)), axis=0)
    held = jnp.concatenate((held, side), axis=1)
    for i in range(ZHS):
        moved = pltpu.roll(held, WIDE - HEAD * i, axis=1) if i else held
        for c in range(2):
            part = jnp.concatenate((moved[HEAD * c:HEAD * (c + 1), 0:128], jnp.zeros((ZROWS - HEAD, 128), F32)), axis=0)
            zs[2 * i + c] = part.astype(BF16)
    slot = core * ZHS + zh
    for k in range(1, 2 * ZHS):
        to_zh, to_core = z_peer(k)
        remote(
            zs.at[2 * to_zh + to_core], zr.at[slot], z_s, z_r, clip=to_zh * YS + y, seq=2 * chip + to_core
        ).start()
    zr[slot] = zs[corner]
    heads(0, HEADS, *spatial)


    writes = []
    for n, (low, top) in enumerate(BACK):
        own_back[n].wait()
        drain(TE.at[:, 0:others, low:top], b_r.at[n])
    for n, ref in enumerate((otq, otk, otv)):
        write = pltpu.make_async_copy(TE.at[n], ref, out_sem.at[n])
        write.start()
        writes.append(write)

    drain(zr.at[0:2 * ZHS - 1], z_r)
    for m, ref in enumerate((ows, owt)):
        four = [zr[ZHS * m + i].astype(F32) for i in range(ZHS)]
        ref[...] = (four[0] + four[1] + four[2] + four[3])[0:HEAD, 0:HEAD]

    drain(X.at[0, 0:others], a_s.at[0])
    for n, (begin, stop) in enumerate(FORWARD):
        drain(X.at[1:4, 0:others, begin:stop], a_s.at[1 + n])
    for n, (low, top) in enumerate(BACK):
        drain(TD.at[:, 0:others, low:top], b_s.at[n])
    for m in range(2):
        drain(W.at[m, 0:(CHIPS - 1) * CHIP_ROWS, 0:128], w1_s.at[m])
        drain(W.at[m, :, 0:256], w2_s.at[m])
        drain(W.at[m, :, 0:128], wf_s.at[m])
        drain(W.at[m, :, 0:512], w3_s.at[m])
    drain(L.at[0:CHIPS - 1, 0:PART], lf_s)
    drain(L.at[0:CHIPS - 1, 0:CHIP_ROWS - YS * PART], lg_s)
    drain(L.at[:, 0:2 * PART], l2_s)
    drain(L.at[:, 0:PART], l4_s)
    drain(W.at[0, :, 0:128], l3_s)
    drain(cen.at[0:others], c_s)
    for k in range(YS):
        drain(psend.at[k], pp_s.at[k])
    for n in range(2):
        drain(yfar.at[n], yf_s.at[n])
        for half in range(2):
            drain(yfar.at[n], y_s.at[half, n])
    drain(xzsend.at[0:(CHIPS - 1) * CHIP_ROWS, 0:256], xz_s)
    drain(rest.at[0:(CHIPS - 1) * REST], xr_s)
    drain(zs.at[0:2 * ZHS - 1], z_s)
    for write in writes:
        write.wait()


def write_out(*refs):
    count = len(refs) // 2 - 2
    sources, targets, sem = refs[:count + 2], refs[count + 2:-1], refs[-1]
    copies = [
        pltpu.make_async_copy(src, dst, sem.at[n])
        for n, (src, dst) in enumerate(zip(sources[:count], targets[:count]))
    ]
    for copy in copies:
        copy.start()
    for src, dst in zip(sources[count:], targets[count:]):
        dst[...] = src[...]
    for copy in copies:
        copy.wait()


def shards(
    space_query, space_keys, space_values, space_output, space_logsum,
    time_query, time_keys, time_values, time_output, time_logsum,
    upstream, space_weight, time_weight,
):
    flat = (S, D)
    dma = pltpu.SemaphoreType.DMA
    big = jax.ShapeDtypeStruct(flat, BF16)
    small = jax.ShapeDtypeStruct((HEAD, HEAD), F32)
    anywhere = pl.BlockSpec(memory_space=pl.ANY)
    held = pl.BlockSpec(memory_space=pltpu.VMEM)
    results = pl.pallas_call(
        kernel,
        out_shape=(pltpu.VMEM(flat, BF16),) * 6 + (pltpu.VMEM((HEAD, HEAD), F32),) * 2,
        in_specs=[anywhere] * 9 + [held] * 4,
        scratch_shapes=[
            pltpu.VMEM((4, S, D), BF16),
            pltpu.VMEM((4, S, D), BF16),
            pltpu.VMEM((2, S, D), BF16),
            pltpu.VMEM((3, S, D), BF16),
            pltpu.VMEM((S, D), BF16),
            pltpu.VMEM((S, D), BF16),
            pltpu.VMEM((3, S, D), BF16),
            pltpu.VMEM((3, S, D), BF16),
            pltpu.VMEM((2, D, D), BF16),
            pltpu.VMEM((CHIPS, CHIP_ROWS, 128), BF16),
            pltpu.VMEM((2, CHIP_ROWS, D), BF16),
            pltpu.VMEM((2, HEAD, D), F32),
            pltpu.VMEM((2, HEAD, D), F32),
            pltpu.VMEM((128, D), BF16),
            pltpu.VMEM((S, S), F32),
            pltpu.VMEM((HEADS, S), F32),
            pltpu.VMEM((S, 128), BF16),
            pltpu.VMEM((S, 128), BF16),
            pltpu.VMEM((128, S), F32),
            pltpu.VMEM((128, S), F32),
            pltpu.VMEM((D, S), F32),
            pltpu.VMEM((YS, YROWS, S), BF16),
            pltpu.VMEM((YS, YROWS, D), F32),
            pltpu.VMEM((YS, YROWS, D), BF16),
            pltpu.VMEM((YS, YROWS, D), BF16),
            pltpu.VMEM((YS - 1, YROWS, D), BF16),
            pltpu.VMEM((2, YROWS // 2, D), BF16),
            pltpu.VMEM((2, YROWS, D), BF16),
            pltpu.VMEM((D, WIDE), BF16),
            pltpu.VMEM((CHIPS - 1, CHIP_ROWS, 256), BF16),
            pltpu.VMEM((CHIPS * REST, 128), BF16),
            pltpu.VMEM((CHIPS - 1, REST, 128), BF16),
            pltpu.VMEM((2 * ZHS, ZROWS, 128), BF16),
            pltpu.VMEM((2 * ZHS, ZROWS, 128), BF16),
            dma((9,)), dma((6,)), dma, dma, dma((2,)), dma((2,)), dma, dma,
            dma, dma, dma, dma((2,)), dma, dma,
            dma((2,)), dma((2, 2)), dma((2,)), dma((2,)), dma((2,)), dma((2,)), dma, dma,
            dma((4,)), dma((4,)), dma, dma, dma((3,)), dma((3,)), dma((4,)), dma((4,)),
            dma((2,)), dma((2,)), dma((2, 2)), dma((2, 2)), dma, dma, dma, dma, dma, dma, dma((3,)),
        ],
        compiler_params=pltpu.CompilerParams(
            collective_id=0, has_side_effects=True, vmem_limit_bytes=60 * 1024 * 1024 - 256 * 1024
        ),
        cost_estimate=pl.CostEstimate(flops=7_000_000_000, bytes_accessed=12_000_000, transcendentals=2_100_000),
    )(
        upstream.reshape(flat), time_query.reshape(flat), time_keys.reshape(flat), time_values.reshape(flat),
        space_output.reshape(flat), time_output.reshape(flat),
        space_query.reshape(flat), space_keys.reshape(flat), space_values.reshape(flat),
        space_weight, time_weight, space_logsum.reshape(HEADS, S), time_logsum.reshape(POS, HEADS, SEQ),
    )
    results = pl.pallas_call(
        write_out,
        out_shape=(big,) * 6 + (small,) * 2,
        in_specs=[anywhere] * 6 + [held] * 2,
        out_specs=(anywhere,) * 6 + (held,) * 2,
        scratch_shapes=[dma((6,))],
        compiler_params=pltpu.CompilerParams(vmem_limit_bytes=1024 * 1024),
    )(*results)
    local = (1, 1, S, D)
    return tuple(result.reshape(local) for result in results[:6]) + tuple(results[6:])


def solution(mesh):
    block = P("clip", "seq", None, None)
    return jax.shard_map(
        shards,
        mesh=mesh,
        in_specs=(block,) * 11 + (P("seq", None),) * 2,
        out_specs=(block,) * 6 + (P("seq", "clip"),) * 2,
        check_vma=False,
    )
```

```python
import math

import jax
import jax.numpy as jnp
from jax import lax
from jax.experimental import pallas as pl
from jax.experimental.pallas import tpu as pltpu
from jax.sharding import PartitionSpec as P

BF16 = jnp.bfloat16
F32 = jnp.float32
HEADS = 16
HEAD = 72
D = HEADS * HEAD
S = 256
SEQ = 16
POS = S // SEQ
CHIPS = 8
YS = 4
ZHS = 4
CHIP_ROWS = 2 * HEAD
YROWS = ZHS * HEAD
WIDE = 384
ZROWS = 80
PART = 32
REST = CHIP_ROWS // 3
GROUPS = ((0, 6), (6, 11), (11, 16))
FORWARD = ((0, 512), (512, 896), (896, 1152))
BACK = ((0, 384), (384, 768), (768, 1152))
NT = (((1,), (1,)), ((), ()))
TN = (((0,), (0,)), ((), ()))
NN = (((1,), (0,)), ((), ()))


def mm(a, b, dims):
    return lax.dot_general(a, b, dims, preferred_element_type=F32)


def kernel(
    up, tq, tk, tv, so, to, sq, sk, sv, ws, wt, slog, tlog,
    osq, osk, osv, otq, otk, otv, ows, owt,
    X, R, O, SI, GT, GS, TD, TE, W, L, wown, w32, w32r,
    ind, bias, tl, cen, cenr, cent, cens,
    ut, utp, mine, psend, prec, ysend, yfar, yrecv, xzsend, xzrecv, rest, restrecv, zs, zr,
    ld, own_sem, wp_s, wp_r, w1_s, w1_r, lf_s, lf_r, lg_s, lg_r, l2_s, l2_r, l4_s, l4_r, w2_s, w2_r, wf_s, wf_r, w3_s, w3_r, l3_s, l3_r,
    a_s, a_r, c_s, c_r, b_s, b_r, pp_s, pp_r, yf_s, yf_r, y_s, y_r, xz_s, xz_r, xr_s, xr_r, z_s, z_r, out_sem,
):
    clip = lax.axis_index("clip")
    seq = lax.axis_index("seq")
    y = lax.rem(clip, YS)
    zh = lax.div(clip, YS)
    core = lax.rem(seq, 2)
    chip = lax.div(seq, 2)
    sibling = seq + 1 - 2 * core
    corner = zh * 2 + core

    def seq_peer(k):
        return lax.rem(seq + k, SEQ)

    def chip_peer(k):
        return 2 * lax.rem(chip + k, CHIPS) + core

    def y_peer(k):
        return zh * YS + lax.rem(y + k, YS)

    def z_peer(k):
        other = lax.rem(corner + k, 2 * ZHS)
        return lax.div(other, 2), lax.rem(other, 2)

    def remote(src, dst, send, recv, **where):
        return pltpu.make_async_remote_copy(
            src_ref=src, dst_ref=dst, send_sem=send, recv_sem=recv,
            device_id=where, device_id_type=pl.DeviceIdType.MESH,
        )

    def drain(ref, sem):
        pltpu.make_async_copy(ref, ref, sem).wait()

    barrier = pltpu.get_barrier_semaphore()
    for k in range(1, SEQ):
        pl.semaphore_signal(barrier, inc=1, device_id={"seq": seq_peer(k)}, device_id_type=pl.DeviceIdType.MESH)
    for k in (1, YS - 1):
        pl.semaphore_signal(barrier, inc=1, device_id={"clip": y_peer(k)}, device_id_type=pl.DeviceIdType.MESH)
    for k in range(1, 2 * ZHS):
        to_zh, to_core = z_peer(k)
        pl.semaphore_signal(
            barrier, inc=1, device_id={"clip": to_zh * YS + y, "seq": 2 * chip + to_core},
            device_id_type=pl.DeviceIdType.MESH,
        )

    loads = [
        pltpu.make_async_copy(src, dst, ld.at[n])
        for n, (src, dst) in enumerate((
            (up, X.at[0]), (tq, X.at[1]), (tk, X.at[2]), (tv, X.at[3]), (so, O.at[0]), (to, O.at[1]),
            (sq, SI.at[0]), (sk, SI.at[1]), (sv, SI.at[2]),
        ))
    ]
    for load in loads:
        load.start()
    w32[0] = wt[...].astype(F32)
    w32[1] = ws[...].astype(F32)

    pl.semaphore_wait(barrier, (SEQ - 1) + 2 + (2 * ZHS - 1))

    pair = remote(w32, w32r, wp_s, wp_r, seq=sibling)
    pair.start()

    loads[0].wait()
    row_me = pl.ds(pl.multiple_of(seq * POS, POS), POS)

    def rows_of(d):
        return pl.ds(pl.multiple_of(d * POS, POS), POS)

    def send_up(k, carry):
        d = seq_peer(k)
        remote(X.at[0, rows_of(d)], R.at[0, row_me], a_s.at[0], a_r.at[0], seq=d).start()
        return carry

    lax.fori_loop(1, SEQ, send_up, 0)
    own_up = pltpu.make_async_copy(X.at[0, row_me], R.at[0, row_me], own_sem.at[0])
    own_up.start()
    for n in range(D // 128):
        ut[128 * n:128 * (n + 1), :] = X[0, :, 128 * n:128 * (n + 1)].astype(F32).T
    pair.wait()
    chip_rows = pl.ds(pl.multiple_of(chip * CHIP_ROWS, 16), CHIP_ROWS)
    tile = pl.ds(pl.multiple_of((2 * y + core) * 128, 128), 128)
    last = pl.ds(D - 128, 128)
    for m in range(2):
        first, second = w32[m], w32r[m]
        low = jnp.where(core == 0, first, second)
        high = jnp.where(core == 0, second, first)
        wown[m] = jnp.concatenate((low, high), axis=0).astype(BF16)
    def stage1(m):
        W[m, chip_rows, tile] = wown[m, :, tile]

        def one(k, carry):
            remote(wown.at[m, :, tile], W.at[m, chip_rows, tile], w1_s.at[m], w1_r.at[m], seq=chip_peer(k)).start()
            return carry

        lax.fori_loop(1, CHIPS, one, 0)

    stage1(0)
    def part_of(k):
        return pl.ds(pl.multiple_of(lax.rem(y + k, YS) * PART, PART), PART)

    part, end_rows = part_of(0), pl.ds(YS * PART, CHIP_ROWS - YS * PART)
    L[chip, part, :] = wown[core, part, last]
    L[chip, end_rows, :] = wown[core, end_rows, last]

    def send_last(k, carry):
        remote(wown.at[core, part, last], L.at[chip, part], lf_s, lf_r, seq=chip_peer(k)).start()
        remote(wown.at[core, end_rows, last], L.at[chip, end_rows], lg_s, lg_r, seq=chip_peer(k)).start()
        return carry

    lax.fori_loop(1, CHIPS, send_last, 0)

    head_row = lax.broadcasted_iota(jnp.int32, (128, D), 0) * HEAD
    column = lax.broadcasted_iota(jnp.int32, (128, D), 1)
    ind[...] = jnp.where((column >= head_row) & (column < head_row + HEAD), 1.0, 0.0).astype(BF16)
    zeros = jnp.zeros((S, D), BF16)
    for n in range(3):
        TD[n] = zeros
    for ref in (osq, osk, osv):
        ref[...] = zeros
    position = lax.broadcasted_iota(jnp.int32, (S, S), 0)
    other = lax.broadcasted_iota(jnp.int32, (S, S), 1)
    bias[...] = jnp.where(lax.rem(position, POS) == lax.rem(other, POS), 0.0, -1e30)

    frame = lax.broadcasted_iota(jnp.int32, (SEQ, S), 0) * POS
    place = lax.broadcasted_iota(jnp.int32, (SEQ, S), 1)
    spread = jnp.zeros((HEADS, S), F32)
    for p in range(POS):
        spread = spread + lax.dot_general(
            tlog[p], jnp.where(place == frame + p, 1.0, 0.0), NN,
            precision=lax.Precision.HIGHEST, preferred_element_type=F32,
        )
    tl[...] = spread

    for j in range(YS):
        utp[j] = jnp.concatenate(
            [ut[HEAD * (YS * i + j):HEAD * (YS * i + j + 1), :] for i in range(ZHS)], axis=0
        ).astype(BF16)
    loads[4].wait()
    loads[5].wait()
    factor = 1.0 / math.sqrt(lax.axis_size("clip") * SEQ * S)

    def gradient(k):
        rows = utp[lax.rem(y + k, YS)]

        def piece(n, carry):
            columns = pl.ds(pl.multiple_of(n * WIDE, 128), WIDE)
            psend[k, :, columns] = (mm(rows, O[1 - core, :, columns], NN) * factor).astype(BF16)
            mine[k, :, columns] = mm(rows, O[core, :, columns], NN) * factor
            return carry

        lax.fori_loop(0, D // WIDE, piece, 0)
        remote(psend.at[k], prec.at[k], pp_s.at[k], pp_r.at[k], seq=sibling).start()

    def tile_of(k):
        return pl.ds(pl.multiple_of((2 * lax.rem(y + k, YS) + core) * 128, 128), 128)

    def to_sibling(m, k):
        remote(W.at[m, :, tile_of(k)], W.at[m, :, tile_of(k)], w3_s.at[m], w3_r.at[m], seq=sibling).start()

    def stage2(m):
        drain(W.at[m, 0:(CHIPS - 1) * CHIP_ROWS, 0:128], w1_r.at[m])
        for n, k in enumerate((1, YS - 1)):
            remote(W.at[m, :, tile], W.at[m, :, tile], w2_s.at[m], w2_r.at[m, n], clip=y_peer(k)).start()
        to_sibling(m, 0)

    def forward2(m):
        for n, k in enumerate((1, YS - 1)):
            drain(W.at[m, :, 0:128], w2_r.at[m, n])
            half = pl.ds(n * (D // 2), D // 2)
            remote(
                W.at[m, half, tile_of(YS - k)], W.at[m, half, tile_of(YS - k)], wf_s.at[m], wf_r.at[m], clip=y_peer(k)
            ).start()
            to_sibling(m, YS - k)

    def stage3(m):
        drain(W.at[m, :, 0:128], wf_r.at[m])
        to_sibling(m, 2)
        drain(W.at[m, :, 0:512], w3_r.at[m])

    near = ((0, 1, 0, YROWS // 2), (1, YS - 1, YROWS // 2, YROWS))

    def far_chunk():
        drain(prec.at[2], pp_r.at[2])
        ysend[1] = (mine[2] + prec[2].astype(F32)).astype(BF16)
        for n, k, low, top in near:
            remote(ysend.at[1, low:top], yfar.at[n], yf_s.at[n], yf_r.at[n], clip=y_peer(k)).start()

    def near_first():
        for n, k, low, top in near:
            rows = slice(YROWS // 2 - low, YROWS // 2 - low + YROWS // 2)
            drain(prec.at[k], pp_r.at[k])
            ysend[k - 1, rows] = (mine[k, rows] + prec[k, rows].astype(F32)).astype(BF16)
            remote(
                ysend.at[k - 1, rows], yrecv.at[n, rows], y_s.at[0, n], y_r.at[0, n], clip=y_peer(k)
            ).start()

    def near_second():
        for n, k, low, top in near:
            rows = slice(low, top)
            drain(yfar.at[n], yf_r.at[n])
            ysend[k - 1, rows] = (
                mine[k, rows] + prec[k, rows].astype(F32) + yfar[n].astype(F32)
            ).astype(BF16)
            remote(
                ysend.at[k - 1, rows], yrecv.at[n, rows], y_s.at[1, n], y_r.at[1, n], clip=y_peer(k)
            ).start()

    def forward(g):
        begin, end = FORWARD[g]
        columns = pl.ds(begin, end - begin)

        def send_group(k, carry):
            d = seq_peer(k)
            remote(
                X.at[1:4, rows_of(d), columns], R.at[1:4, row_me, columns], a_s.at[1 + g], a_r.at[1 + g], seq=d
            ).start()
            return carry

        lax.fori_loop(1, SEQ, send_group, 0)

    gradient(2)
    gradient(1)
    far_chunk()
    stage2(0)
    drain(L.at[0:CHIPS - 1, 0:PART], lf_r)
    for n, k in enumerate((1, YS - 1)):
        remote(L.at[:, part], L.at[:, part], l2_s, l2_r.at[n], clip=y_peer(k)).start()
    for n in (1, 2, 3):
        loads[n].wait()
    forward(0)
    stage1(1)
    forward(1)
    own_rest = pltpu.make_async_copy(X.at[1:4, row_me], R.at[1:4, row_me], own_sem.at[1])
    own_rest.start()
    gradient(3)
    forward2(0)
    for n, k in enumerate((1, YS - 1)):
        drain(L.at[:, 0:PART], l2_r.at[n])
        there = L.at[pl.ds(n * (CHIPS // 2), CHIPS // 2), part_of(YS - k)]
        remote(there, there, l4_s, l4_r, clip=y_peer(k)).start()
    near_first()
    near_second()
    drain(L.at[:, 0:PART], l4_r)
    drain(L.at[0:CHIPS - 1, 0:CHIP_ROWS - YS * PART], lg_r)
    W[core, :, last] = L[...].reshape(D, 128)
    remote(W.at[core, :, last], W.at[core, :, last], l3_s, l3_r, seq=sibling).start()

    stage3(0)
    drain(W.at[0, :, last], l3_r)

    def project(tokens, m, n):
        return mm(tokens, W[m, n * WIDE:(n + 1) * WIDE, :], NT).astype(BF16)

    def split(grad, outputs):
        product = grad.astype(F32) * outputs.astype(F32)
        high = product.astype(BF16)
        return high, (product - high.astype(F32)).astype(BF16)

    total = jnp.zeros((S, 128), F32)
    for n in range(D // WIDE):
        columns = slice(n * WIDE, (n + 1) * WIDE)
        high, low = split(project(X[0], 0, n), O[1, :, columns])
        total = total + (mm(high, ind[:, columns], NT) + mm(low, ind[:, columns], NT))
    high = total.astype(BF16).astype(F32)
    cen[...] = (high + pltpu.roll(total - high, HEADS, axis=1)).astype(BF16)

    def send_center(k, carry):
        d = seq_peer(k)
        remote(cen.at[rows_of(d)], cenr.at[row_me], c_s, c_r, seq=d).start()
        return carry

    lax.fori_loop(1, SEQ, send_center, 0)
    own_cen = pltpu.make_async_copy(cen.at[row_me], cenr.at[row_me], own_sem.at[2])
    own_cen.start()
    forward(2)

    others = (SEQ - 1) * POS
    own_up.wait()
    drain(R.at[0, 0:others], a_r.at[0])
    for n in range(D // WIDE):
        GT[:, n * WIDE:(n + 1) * WIDE] = project(R[0], 0, n)
    gradient(0)
    own_cen.wait()
    drain(cenr.at[0:others], c_r)
    both = cenr[...].astype(F32)
    cent[...] = (both + pltpu.roll(both, 128 - HEADS, axis=1)).T

    scale = 1.0 / math.sqrt(HEAD)
    lane = lax.broadcasted_iota(jnp.int32, (16, 256), 1)

    def heads(first, end, q_ref, k_ref, v_ref, g_ref, log_ref, center_ref, masked, out):
        def one(h, carry):
            offset = jnp.minimum(lax.div(h * HEAD, 128), D // 128 - 2) * 128
            window = pl.ds(pl.multiple_of(offset, 128), 256)
            begin = h * HEAD - offset
            keep = jnp.where((lane >= begin) & (lane < begin + HEAD), 1.0, 0.0).astype(BF16)
            keep = jnp.broadcast_to(keep[None], (S // 16, 16, 256)).reshape(S, 256)
            q = q_ref[:, window] * keep
            g = g_ref[:, window] * keep
            k = k_ref[:, window]
            v = v_ref[:, window]
            scores = mm(k, q, NT) * scale - log_ref[pl.ds(h, 1), :]
            if masked:
                scores = scores + bias[...]
            probs = jnp.exp(scores)
            dscore = (probs * (mm(v, g, NT) - center_ref[pl.ds(h, 1), :]) * scale).astype(BF16)
            out[0][:, window] = out[0][:, window] + mm(dscore, k * keep, TN).astype(BF16)
            out[1][:, window] = out[1][:, window] + mm(dscore, q, NN).astype(BF16)
            out[2][:, window] = out[2][:, window] + mm(probs.astype(BF16), g, NN).astype(BF16)
            return carry

        lax.fori_loop(first, end, one, 0, unroll=2 if (end - first) % 2 == 0 else 1)

    def over_chips():
        drain(prec.at[0], pp_r.at[0])
        for n in range(2):
            for half in range(2):
                drain(yrecv.at[n, 0:YROWS // 2], y_r.at[half, n])
        for n in range(D // 128):
            columns = slice(128 * n, 128 * (n + 1))
            held = mine[0, :, columns] + prec[0, :, columns].astype(F32)
            for n_from in range(2):
                held = held + yrecv[n_from, :, columns].astype(F32)
            held = jnp.concatenate((held, jnp.zeros((WIDE - YROWS, 128), F32)), axis=0)
            xzsend[128 * n:128 * (n + 1), :] = held.T.astype(BF16)
        for c in range(CHIPS):
            parts = [
                xzsend[CHIP_ROWS * c + REST * g:CHIP_ROWS * c + REST * (g + 1), 256:WIDE].astype(F32)
                for g in range(3)
            ]
            rest[REST * c:REST * (c + 1), :] = (
                parts[0] + pltpu.roll(parts[1], 32, axis=1) + pltpu.roll(parts[2], 64, axis=1)
            ).astype(BF16)
        for k in range(1, CHIPS):
            to_chip = lax.rem(chip + k, CHIPS)
            there = pl.ds(pl.multiple_of(to_chip * CHIP_ROWS, 16), CHIP_ROWS)
            remote(xzsend.at[there, 0:256], xzrecv.at[k - 1], xz_s, xz_r, seq=chip_peer(k)).start()
            there = pl.ds(pl.multiple_of(to_chip * REST, 16), REST)
            remote(rest.at[there], restrecv.at[k - 1], xr_s, xr_r, seq=chip_peer(k)).start()

    own_rest.wait()
    own_back = []
    for n, ((first, end), (begin, stop), (low, top)) in enumerate(zip(GROUPS, FORWARD, BACK)):
        drain(R.at[1:4, 0:others, begin:stop], a_r.at[1 + n])
        heads(first, end, R.at[1], R.at[2], R.at[3], GT, tl, cent, True, [TD.at[m] for m in range(3)])
        columns = pl.ds(low, top - low)

        def send_back(k, carry, n=n, columns=columns):
            d = seq_peer(k)
            remote(TD.at[:, rows_of(d), columns], TE.at[:, row_me, columns], b_s.at[n], b_r.at[n], seq=d).start()
            return carry

        lax.fori_loop(1, SEQ, send_back, 0)
        back = pltpu.make_async_copy(TD.at[:, row_me, columns], TE.at[:, row_me, columns], own_sem.at[3 + n])
        back.start()
        own_back.append(back)
        if n == 0:
            over_chips()
            stage2(1)
        elif n == 1:
            forward2(1)

    stage3(1)
    total = jnp.zeros((128, S), F32)
    for n in range(D // WIDE):
        columns = slice(n * WIDE, (n + 1) * WIDE)
        grad = project(X[0], 1, n)
        GS[:, columns] = grad
        high, low = split(grad, O[0, :, columns])
        total = total + (mm(ind[:, columns], high, NT) + mm(ind[:, columns], low, NT))
    cens[...] = total
    for n in (6, 7, 8):
        loads[n].wait()
    spatial = (SI.at[0], SI.at[1], SI.at[2], GS, slog, cens, False, (osq, osk, osv))
    drain(xzrecv, xz_r)
    drain(restrecv, xr_r)
    held = xzsend[chip_rows, 0:256].astype(F32)
    side = rest[pl.ds(pl.multiple_of(chip * REST, 16), REST), :].astype(F32)
    for k in range(CHIPS - 1):
        held = held + xzrecv[k].astype(F32)
        side = side + restrecv[k].astype(F32)
    side = jnp.concatenate((side, pltpu.roll(side, 96, axis=1), pltpu.roll(side, 64, axis=1)), axis=0)
    held = jnp.concatenate((held, side), axis=1)
    for i in range(ZHS):
        moved = pltpu.roll(held, WIDE - HEAD * i, axis=1) if i else held
        for c in range(2):
            part = jnp.concatenate((moved[HEAD * c:HEAD * (c + 1), 0:128], jnp.zeros((ZROWS - HEAD, 128), F32)), axis=0)
            zs[2 * i + c] = part.astype(BF16)
    slot = core * ZHS + zh
    for k in range(1, 2 * ZHS):
        to_zh, to_core = z_peer(k)
        remote(
            zs.at[2 * to_zh + to_core], zr.at[slot], z_s, z_r, clip=to_zh * YS + y, seq=2 * chip + to_core
        ).start()
    zr[slot] = zs[corner]
    heads(0, HEADS, *spatial)


    writes = []
    for n, (low, top) in enumerate(BACK):
        own_back[n].wait()
        drain(TE.at[:, 0:others, low:top], b_r.at[n])
    for n, ref in enumerate((otq, otk, otv)):
        write = pltpu.make_async_copy(TE.at[n], ref, out_sem.at[n])
        write.start()
        writes.append(write)

    drain(zr.at[0:2 * ZHS - 1], z_r)
    for m, ref in enumerate((ows, owt)):
        four = [zr[ZHS * m + i].astype(F32) for i in range(ZHS)]
        ref[...] = (four[0] + four[1] + four[2] + four[3])[0:HEAD, 0:HEAD]

    drain(X.at[0, 0:others], a_s.at[0])
    for n, (begin, stop) in enumerate(FORWARD):
        drain(X.at[1:4, 0:others, begin:stop], a_s.at[1 + n])
    for n, (low, top) in enumerate(BACK):
        drain(TD.at[:, 0:others, low:top], b_s.at[n])
    for m in range(2):
        drain(W.at[m, 0:(CHIPS - 1) * CHIP_ROWS, 0:128], w1_s.at[m])
        drain(W.at[m, :, 0:256], w2_s.at[m])
        drain(W.at[m, :, 0:128], wf_s.at[m])
        drain(W.at[m, :, 0:512], w3_s.at[m])
    drain(L.at[0:CHIPS - 1, 0:PART], lf_s)
    drain(L.at[0:CHIPS - 1, 0:CHIP_ROWS - YS * PART], lg_s)
    drain(L.at[:, 0:2 * PART], l2_s)
    drain(L.at[:, 0:PART], l4_s)
    drain(W.at[0, :, 0:128], l3_s)
    drain(cen.at[0:others], c_s)
    for k in range(YS):
        drain(psend.at[k], pp_s.at[k])
    for n in range(2):
        drain(yfar.at[n], yf_s.at[n])
        for half in range(2):
            drain(yfar.at[n], y_s.at[half, n])
    drain(xzsend.at[0:(CHIPS - 1) * CHIP_ROWS, 0:256], xz_s)
    drain(rest.at[0:(CHIPS - 1) * REST], xr_s)
    drain(zs.at[0:2 * ZHS - 1], z_s)
    for write in writes:
        write.wait()


def write_out(*refs):
    count = len(refs) // 2 - 2
    sources, targets, sem = refs[:count + 2], refs[count + 2:-1], refs[-1]
    copies = [
        pltpu.make_async_copy(src, dst, sem.at[n])
        for n, (src, dst) in enumerate(zip(sources[:count], targets[:count]))
    ]
    for copy in copies:
        copy.start()
    for src, dst in zip(sources[count:], targets[count:]):
        dst[...] = src[...]
    for copy in copies:
        copy.wait()


def shards(
    space_query, space_keys, space_values, space_output, space_logsum,
    time_query, time_keys, time_values, time_output, time_logsum,
    upstream, space_weight, time_weight,
):
    flat = (S, D)
    dma = pltpu.SemaphoreType.DMA
    big = jax.ShapeDtypeStruct(flat, BF16)
    small = jax.ShapeDtypeStruct((HEAD, HEAD), F32)
    anywhere = pl.BlockSpec(memory_space=pl.ANY)
    held = pl.BlockSpec(memory_space=pltpu.VMEM)
    results = pl.pallas_call(
        kernel,
        out_shape=(pltpu.VMEM(flat, BF16),) * 6 + (pltpu.VMEM((HEAD, HEAD), F32),) * 2,
        in_specs=[anywhere] * 9 + [held] * 4,
        scratch_shapes=[
            pltpu.VMEM((4, S, D), BF16),
            pltpu.VMEM((4, S, D), BF16),
            pltpu.VMEM((2, S, D), BF16),
            pltpu.VMEM((3, S, D), BF16),
            pltpu.VMEM((S, D), BF16),
            pltpu.VMEM((S, D), BF16),
            pltpu.VMEM((3, S, D), BF16),
            pltpu.VMEM((3, S, D), BF16),
            pltpu.VMEM((2, D, D), BF16),
            pltpu.VMEM((CHIPS, CHIP_ROWS, 128), BF16),
            pltpu.VMEM((2, CHIP_ROWS, D), BF16),
            pltpu.VMEM((2, HEAD, D), F32),
            pltpu.VMEM((2, HEAD, D), F32),
            pltpu.VMEM((128, D), BF16),
            pltpu.VMEM((S, S), F32),
            pltpu.VMEM((HEADS, S), F32),
            pltpu.VMEM((S, 128), BF16),
            pltpu.VMEM((S, 128), BF16),
            pltpu.VMEM((128, S), F32),
            pltpu.VMEM((128, S), F32),
            pltpu.VMEM((D, S), F32),
            pltpu.VMEM((YS, YROWS, S), BF16),
            pltpu.VMEM((YS, YROWS, D), F32),
            pltpu.VMEM((YS, YROWS, D), BF16),
            pltpu.VMEM((YS, YROWS, D), BF16),
            pltpu.VMEM((YS - 1, YROWS, D), BF16),
            pltpu.VMEM((2, YROWS // 2, D), BF16),
            pltpu.VMEM((2, YROWS, D), BF16),
            pltpu.VMEM((D, WIDE), BF16),
            pltpu.VMEM((CHIPS - 1, CHIP_ROWS, 256), BF16),
            pltpu.VMEM((CHIPS * REST, 128), BF16),
            pltpu.VMEM((CHIPS - 1, REST, 128), BF16),
            pltpu.VMEM((2 * ZHS, ZROWS, 128), BF16),
            pltpu.VMEM((2 * ZHS, ZROWS, 128), BF16),
            dma((9,)), dma((6,)), dma, dma, dma((2,)), dma((2,)), dma, dma,
            dma, dma, dma, dma((2,)), dma, dma,
            dma((2,)), dma((2, 2)), dma((2,)), dma((2,)), dma((2,)), dma((2,)), dma, dma,
            dma((4,)), dma((4,)), dma, dma, dma((3,)), dma((3,)), dma((4,)), dma((4,)),
            dma((2,)), dma((2,)), dma((2, 2)), dma((2, 2)), dma, dma, dma, dma, dma, dma, dma((3,)),
        ],
        compiler_params=pltpu.CompilerParams(
            collective_id=0, has_side_effects=True, vmem_limit_bytes=60 * 1024 * 1024 - 256 * 1024
        ),
        cost_estimate=pl.CostEstimate(flops=7_000_000_000, bytes_accessed=12_000_000, transcendentals=2_100_000),
    )(
        upstream.reshape(flat), time_query.reshape(flat), time_keys.reshape(flat), time_values.reshape(flat),
        space_output.reshape(flat), time_output.reshape(flat),
        space_query.reshape(flat), space_keys.reshape(flat), space_values.reshape(flat),
        space_weight, time_weight, space_logsum.reshape(HEADS, S), time_logsum.reshape(POS, HEADS, SEQ),
    )
    results = pl.pallas_call(
        write_out,
        out_shape=(big,) * 6 + (small,) * 2,
        in_specs=[anywhere] * 6 + [held] * 2,
        out_specs=(anywhere,) * 6 + (held,) * 2,
        scratch_shapes=[dma((6,))],
        compiler_params=pltpu.CompilerParams(vmem_limit_bytes=1024 * 1024),
    )(*results)
    local = (1, 1, S, D)
    return tuple(result.reshape(local) for result in results[:6]) + tuple(results[6:])


def solution(mesh):
    block = P("clip", "seq", None, None)
    return jax.shard_map(
        shards,
        mesh=mesh,
        in_specs=(block,) * 11 + (P("seq", None),) * 2,
        out_specs=(block,) * 6 + (P("seq", "clip"),) * 2,
        check_vma=False,
    )
```
